1024 devices in a mesh: ctx: 16 (over z), exp: 64 (over y, x, core).
Axes of the slice: x: 4, y: 8, z: 16, core: 2. Of those that a mesh axis runs over, the one named last changes fastest.
Arguments:
- queries: bfloat16 [2048, 8192], P('ctx', 'exp'), may hold values from -30 to 30
- keyvals: bfloat16 [2, 2048, 512], P(None, 'ctx'), may hold values from -7 to 7
- d_attn: bfloat16 [2048, 8192], P('ctx', 'exp'), may hold values from -6 to 6
- grad_tokens: bfloat16 [8192, 4096], P(('ctx', 'exp')), may hold values from -6 to 6
- expert_ids: int32 [8192, 8], P(('ctx', 'exp')), may hold values from 0 to 63, all different within a row; in each aligned block of 8 rows (0 to 7, 8 to 15, ...) at most 2 rows name the same one
- route_weights: float32 [8192, 8], P(('ctx', 'exp')), may hold values from 0.05 to 0.3
- saved_gate_up: bfloat16 [16, 64, 128, 1536], P('ctx', 'exp'), may hold values from -6 to 6
- down_weight: bfloat16 [64, 768, 4096], P('exp'), may hold values from -0.21875 to 0.21875
Outputs:
- d_queries: bfloat16 [2048, 8192], P('ctx', 'exp')
- d_keyvals: float32 [2048, 4, 256], P(('ctx', 'exp'))
- d_gate_up: bfloat16 [16, 64, 128, 1536], P('ctx', 'exp')
The draws below stay inside these ranges and needn't reach their ends.
Inputs may be any that keep to these rules, and one draw needn't show every extreme that they name: `expert_ids`: each row names 8 different experts; among the rows of one device no expert is named more than 2 times.
All inputs are finite; a program needn't handle non-finite values.
Results may differ from the reference program's by a relative error of at most 0.011.
Values may be sent and summed in bfloat16 or wider, within the bound.
A program may use at most 32 MiB of HBM per device.

```python
import math
import jax
import jax.numpy as jnp
import numpy as np
from jax import lax

D = 4096
HEAD = 128
KV = 4
TOP = 8
FF = 768
TOKX = 8
HEADS = 64
EXPERTS = 64
CAP = 2
SLOTS = 128
LEN = 2048
XROWS = 8192
N_CTX = 16


def lifted_rows(count):
    positions = jnp.arange(count)
    special = positions % 97 == 5
    strength = 14.0 + 8.0 * (positions // 97 % 3).astype(jnp.float32)
    return (special, strength)


def shared_keys(key, lift):
    keys = jnp.clip(jax.random.normal(key, (LEN, KV * HEAD), jnp.float32), -6.0, 6.0)
    special, strength = lifted_rows(LEN)
    following = jnp.roll(keys, -1, axis=0)
    strength_next = jnp.roll(strength, -1)
    special_next = jnp.roll(special, -1)
    step_size = 2.0 * math.sqrt(HEAD) / (HEAD * strength_next)
    lowered = following - step_size[:, None] * jnp.sign(following)
    return jnp.where((special_next & (lift > 0.0))[:, None], lowered, keys)


def draw_keyvals(key, part):
    keys = shared_keys(key, 0.0)
    key = jax.random.fold_in(key, 3)
    values = jnp.clip(jax.random.normal(key, (LEN, KV * HEAD), jnp.float32), -6.0, 6.0)
    return jnp.stack([keys, values]).astype(jnp.bfloat16)


def draw_queries(key, part):
    key = jax.random.fold_in(key, 5)
    result = jnp.clip(jax.random.normal(key, (LEN, HEADS * HEAD), jnp.float32), -6.0, 6.0)
    return result.astype(jnp.bfloat16)


def shard_levels(stream_key, shape, shards, least, largest):
    level = 1.0
    for dim, blocks in shards:
        heights = jax.random.uniform(jax.random.fold_in(jax.random.fold_in(stream_key, 6), dim), (blocks,), jnp.float32, least / len(shards), largest / len(shards))
        level = level * jnp.repeat(jnp.exp(heights), shape[dim] // blocks).reshape((-1,) + (1,) * (len(shape) - 1 - dim))
    return level


def deal_out(rng, own, number, rows, number_of, top, limit, lean):
    sequence = jax.random.permutation(rng, number_of)
    crowded, common = portions_of(number_of, rows * top, limit, lean, True), portions_of(number_of, rows * top, limit, lean, False)
    places = jnp.arange(number_of)

    def named(tallies, rotation):
        used = int((tallies > 0).sum())
        fixed = max(1, used // 4)
        shifted = fixed + (places - fixed + rotation * (used - fixed)) % max(1, number_of - fixed)
        return jnp.zeros((number_of,), jnp.int32).at[sequence[jnp.where(places < fixed, places, shifted)]].set(jnp.asarray(tallies, jnp.int32))

    tallies = jnp.where(number % 4 == 0, named(crowded, number // 4), named(common, number - number // 4 - 1))
    mixed = jax.random.permutation(jax.random.fold_in(own, 3), number_of)
    giver, taker = mixed[0:number_of // 2 * 2:2], mixed[1:number_of // 2 * 2:2]
    room = jnp.minimum(tallies[giver] - 1, limit - tallies[taker]) // 2
    room = jnp.where((giver == sequence[0]) | (taker == sequence[0]) | (tallies[taker] == 0), 0, jnp.maximum(room, 0))
    shifted = jax.random.randint(jax.random.fold_in(own, 4), (number_of // 2,), 0, 1 << 20) % (room + 1)
    tallies = tallies.at[giver].add(-shifted).at[taker].add(shifted)
    members = jnp.searchsorted(jnp.cumsum(tallies), jnp.arange(rows * top), side="right").astype(jnp.int32)
    listing = members.reshape(top, rows).T
    listing = listing[jax.random.permutation(jax.random.fold_in(own, 1), rows)]
    rotation = jax.random.randint(jax.random.fold_in(own, 2), (rows, 1), 0, top)
    return jnp.take_along_axis(listing, (jnp.arange(top)[None, :] + rotation) % top, axis=1)


def portions_of(number_of, total, bound, slope, full):
    portions = [(1 << 20) // math.isqrt(rank ** slope) + 1 for rank in range(1, number_of + 1)]
    largest = bound if full else min(bound, max(-(-total // number_of), total * portions[0] // sum(portions)))
    least = 1 if total - largest >= number_of - 1 else 0
    given, surplus = [largest] + [least] * (number_of - 1), total - largest - least * (number_of - 1)
    while surplus > 0:
        candidates = [i for i in range(1, number_of) if given[i] < largest] or [i for i in range(1, number_of) if given[i] < bound]
        mass, left = sum([portions[i] for i in candidates]), surplus
        for i in candidates:
            more = min(bound - given[i], max(1, left * portions[i] // mass), surplus)
            given[i] = given[i] + more
            surplus = surplus - more
    return np.array(given)


def centred(key, extent, width, bound, split=(), held_as=jnp.bfloat16):
    entries = jax.random.normal(key, extent, jnp.float32) * width
    if len(split) > 0:
        entries = shard_levels(key, extent, split, -0.22, 0.18) * entries
    return jnp.clip(entries, min=-bound, max=bound).astype(held_as)


def setup_inputs(seed: int = 0) -> dict:
    seeds = jax.random.split(jax.random.key(seed), 9)
    queries = draw_queries(jax.random.fold_in(seeds[8], 71), 0)
    keyvals = draw_keyvals(jax.random.fold_in(seeds[8], 71), 0)
    d_attn = centred(seeds[2], (LEN, HEADS * HEAD), 1.0, 6.0, ((0, 16), (1, 64)))
    grad_tokens = centred(seeds[3], (XROWS, D), 1.0, 6.0, ((0, 1024),))
    expert_ids_keys = jax.random.split(jax.random.fold_in(seeds[4], 1), XROWS // TOKX)
    expert_ids_turns = jax.random.permutation(jax.random.fold_in(seeds[4], 3), XROWS // TOKX)
    expert_ids = jax.vmap(lambda own, number: deal_out(jax.random.fold_in(seeds[4], 2), own, number, TOKX, EXPERTS, TOP, CAP, 2))(expert_ids_keys, expert_ids_turns).reshape((XROWS, TOP))
    route_weights = jnp.clip(0.05 + 0.25 * jax.random.uniform(seeds[5], (XROWS, TOP), jnp.float32) ** shard_levels(seeds[5], (XROWS, TOP), ((0, 1024),), -0.2, 0.2), 0.05, 0.3)
    saved_gate_up = centred(seeds[6], (N_CTX, EXPERTS, SLOTS, 2 * FF), 1.0, 6.0, ((0, 16), (1, 64)))
    down_weight = centred(seeds[7], (EXPERTS, FF, D), FF ** -0.5, 0.21875, ((0, 64),))
    return dict(queries=queries, keyvals=keyvals, d_attn=d_attn, grad_tokens=grad_tokens, expert_ids=expert_ids, route_weights=route_weights, saved_gate_up=saved_gate_up, down_weight=down_weight)


def head_terms(query_head, grad_head, key_head, value_head):
    length = query_head.shape[0]
    score_scale = 1.0 / math.sqrt(HEAD)
    positions = jnp.arange(length)
    causal = positions[None, :] <= positions[:, None]
    scores = jnp.dot(query_head, key_head.T, preferred_element_type=jnp.float32) * score_scale
    scores = jnp.where(causal, scores, -jnp.inf)
    highest = lax.optimization_barrier(jnp.max(scores, axis=1, keepdims=True))
    log_total = highest[:, 0] + jnp.log(lax.optimization_barrier(jnp.sum(jnp.exp(scores - highest), axis=1)))
    softmax = jnp.exp(scores - log_total[:, None])
    softmax_b = softmax.astype(jnp.bfloat16)
    attended = jnp.dot(softmax_b, value_head, preferred_element_type=jnp.float32)
    row_delta = lax.optimization_barrier(jnp.sum(grad_head.astype(jnp.float32) * attended, axis=1))
    d_softmax = jnp.dot(grad_head, value_head.T, preferred_element_type=jnp.float32)
    d_scores = (softmax * (d_softmax - row_delta[:, None])).astype(jnp.bfloat16)
    d_query = (jnp.dot(d_scores, key_head, preferred_element_type=jnp.float32) * score_scale).astype(jnp.bfloat16)
    key_grad = jnp.dot(d_scores.T, query_head, preferred_element_type=jnp.float32) * score_scale
    value_grad = jnp.dot(softmax_b.T, grad_head, preferred_element_type=jnp.float32)
    return (d_query, jnp.concatenate([key_grad, value_grad], axis=1))

def expert_group(items, down_weight):
    tokens_group, ids_group, weights_group, stored_group = items
    chosen = (ids_group[..., None] == jnp.arange(EXPERTS, dtype=jnp.int32)).astype(jnp.int32)
    per_row = lax.optimization_barrier(jnp.sum(chosen, axis=2))
    before = jnp.cumsum(per_row, axis=1) - per_row
    slot_index = lax.optimization_barrier(jnp.sum(chosen * before[:, :, None, :], axis=3)).astype(jnp.int32)
    source = jnp.arange(EXPERTS, dtype=jnp.int32)[:, None, None]
    flat_slot = (source * CAP + slot_index).astype(jnp.int32)
    scaled = (weights_group[..., None] * tokens_group.astype(jnp.float32)[:, :, None, :]).astype(jnp.bfloat16)
    received = jnp.zeros((EXPERTS, SLOTS, D), jnp.bfloat16)
    received = received.at[ids_group.reshape(-1), flat_slot.reshape(-1)].set(scaled.reshape(-1, D))

    def per_expert(pair):
        rows_expert, weight_expert = pair
        return jnp.dot(rows_expert, weight_expert.T, preferred_element_type=jnp.float32)
    d_hidden = lax.map(per_expert, (received, down_weight))
    stored = stored_group.astype(jnp.float32)
    gate_part = stored[..., :FF]
    up_part = stored[..., FF:]
    sigmoid_gate = 1.0 / (1.0 + jnp.exp(-gate_part))
    d_gate = d_hidden * up_part * sigmoid_gate * (1.0 + gate_part * (1.0 - sigmoid_gate))
    d_up = d_hidden * gate_part * sigmoid_gate
    return jnp.concatenate([d_gate, d_up], axis=-1).astype(jnp.bfloat16)

def reference(queries, keyvals, d_attn, grad_tokens, expert_ids, route_weights, saved_gate_up, down_weight):
    query_heads = queries.reshape(LEN, HEADS, HEAD).transpose(1, 0, 2)
    grad_heads = d_attn.reshape(LEN, HEADS, HEAD).transpose(1, 0, 2)
    pair_heads = keyvals.reshape(2, LEN, KV, HEAD).transpose(2, 0, 1, 3)
    head_groups = (jnp.arange(HEADS, dtype=jnp.int32) // (HEADS // KV)).astype(jnp.int32)

    def per_head(items):
        query_head, grad_head, kv_group = items
        pair = lax.dynamic_index_in_dim(pair_heads, kv_group, 0, keepdims=False)
        return head_terms(query_head, grad_head, pair[0], pair[1])
    d_heads, key_terms = lax.map(per_head, (query_heads, grad_heads, head_groups))
    d_queries = d_heads.transpose(1, 0, 2).reshape(LEN, HEADS * HEAD)
    d_keyvals = lax.optimization_barrier(jnp.sum(key_terms.reshape(KV, HEADS // KV, LEN, 2 * HEAD), axis=1)).transpose(1, 0, 2)
    tokens_all = grad_tokens.reshape(N_CTX, EXPERTS, TOKX, D)
    ids_all = expert_ids.reshape(N_CTX, EXPERTS, TOKX, TOP)
    weights_all = route_weights.reshape(N_CTX, EXPERTS, TOKX, TOP)
    d_gate_up = lax.map(lambda items: expert_group(items, down_weight), (tokens_all, ids_all, weights_all, saved_gate_up))
    return (d_queries, d_keyvals, d_gate_up)
```

```python
import math

import jax
import jax.numpy as jnp
from jax import lax
from jax.experimental import pallas as pl
from jax.experimental.pallas import tpu as pltpu
from jax.sharding import PartitionSpec as P

MESH = pl.DeviceIdType.MESH
F32, BF16, I32 = jnp.float32, jnp.bfloat16, jnp.int32

NZ = 16
NE = 64
NX = 4
NY = 8
ROWS = 128
HEAD = 128
SUB = ROWS // NX
KEYS = NZ * SUB
HALF = SUB // 2
FF = 768
CH = 512
NQ = 8
MSG = 2 * NQ
SLOTS = 2 * NE
MASKED = -1e30

contract_last = (((1,), (1,)), ((), ()))
contract_first = (((0,), (0,)), ((), ()))


def send(src, dst, ss, rs, device):
    return pltpu.make_async_remote_copy(
        src_ref=src, dst_ref=dst, send_sem=ss, recv_sem=rs, device_id=device, device_id_type=MESH
    )


def route_matrix(ids_ref, wts_ref):
    ids = ids_ref[...].astype(F32)
    wts = wts_ref[...]
    col = lax.broadcasted_iota(I32, (8, 128), 1)
    tok = lax.broadcasted_iota(I32, (8, 128), 0)
    col_tok = lax.rem(col, 8)
    chunk = (lax.rem(col, 64) // 8)[0:1]
    low = col[0:1] >= 64
    pick = col_tok == tok
    earlier = tok < col_tok
    spread = []
    for k in range(8):
        spread.append(jnp.broadcast_to(ids[:, k : k + 1], (8, 128)))
    row = lax.broadcasted_iota(I32, (SLOTS * NQ, 128), 0)
    total = jnp.zeros((SLOTS * NQ, 128), F32)
    for k in range(8):
        named = jnp.sum(jnp.where(pick, spread[k], 0.0), axis=0, keepdims=True)
        weight = jnp.sum(
            jnp.where(pick, jnp.broadcast_to(wts[:, k : k + 1], (8, 128)), 0.0),
            axis=0,
            keepdims=True,
        )
        count = jnp.zeros((8, 128), F32)
        for other in range(8):
            count += jnp.where(earlier & (spread[other] == named), 1.0, 0.0)
        slot = jnp.sum(count, axis=0, keepdims=True)
        code = (named * (2 * NQ) + slot * NQ).astype(I32) + chunk
        high = weight.astype(BF16).astype(F32)
        part = jnp.where(low, weight - high, high)
        total += jnp.where(row == code, part, 0.0)
    return total.astype(BF16)


def kernel(
    q_ref, kv_ref, do_ref, tok_ref, ids_ref, wts_ref, saved_ref, down_ref,
    dq_out, dkv_out, dgu_out,
    qd, kv, pun, dps, stats, dqs, dqr, acc, halves, core_in, zs, zr, fs, fr,
    tok_v, ids_v, wts_v, saved_v, down_v, outgoing, incoming,
    loc, kv_ss, kv_rs, x_ss, x_rs, st_ss, st_rs, dq_ss, dq_rs, c_ss, c_rs,
    z_ss, z_rs, f_ss, f_rs, a_ss, a_rs,
):
    z, e = lax.axis_index("ctx"), lax.axis_index("exp")
    c = lax.rem(e, 2)
    x = lax.rem(e // 2, NX)
    y = e // (2 * NX)
    g = y // 2
    scale = 1.0 / math.sqrt(HEAD)
    partner = {"ctx": z, "exp": e + 1 - 2 * c}

    def x_peer(k):
        other = lax.rem(x + k, NX)
        return other, {"ctx": z, "exp": y * (2 * NX) + other * 2 + c}

    kv[...] = jnp.zeros_like(kv)
    zr[...] = jnp.zeros_like(zr)
    barrier = pltpu.get_barrier_semaphore()

    @pl.loop(1, NZ)
    def _(k):
        pl.semaphore_signal(
            barrier, inc=1, device_id={"ctx": lax.rem(z + k, NZ), "exp": e}, device_id_type=MESH
        )

    @pl.loop(1, NE)
    def _(k):
        pl.semaphore_signal(
            barrier, inc=1, device_id={"ctx": z, "exp": lax.rem(e + k, NE)}, device_id_type=MESH
        )

    local = [
        pltpu.make_async_copy(
            kv_ref.at[c, pl.ds(x * SUB, SUB), pl.ds(g * HEAD, HEAD)], kv.at[c, z], loc.at[0]
        ),
        pltpu.make_async_copy(q_ref, qd.at[x, 0], loc.at[1]),
        pltpu.make_async_copy(do_ref, qd.at[x, 1], loc.at[2]),
        pltpu.make_async_copy(tok_ref, tok_v, loc.at[3]),
        pltpu.make_async_copy(ids_ref, ids_v, loc.at[4]),
        pltpu.make_async_copy(wts_ref, wts_v, loc.at[5]),
        pltpu.make_async_copy(saved_ref.at[0, 0], saved_v, loc.at[6]),
        pltpu.make_async_copy(down_ref.at[0], down_v, loc.at[7]),
    ]
    for copy in local:
        copy.start()
    for copy in local[:6]:
        copy.wait()

    wide = tok_v[...].astype(F32)
    chunks = [wide[:, n * CH : (n + 1) * CH] for n in range(NQ)]
    tokens = jnp.concatenate(chunks + chunks, axis=0).astype(BF16)
    outgoing[...] = jnp.dot(
        route_matrix(ids_v, wts_v), tokens, preferred_element_type=F32
    ).astype(BF16)

    pl.semaphore_wait(barrier, NZ - 1 + NE - 1)

    @pl.loop(1, NZ)
    def _(k):
        to = NZ - k

        @pl.when(to > z)
        def _():
            send(
                kv.at[c, z], kv.at[c, z], kv_ss.at[to], kv_rs.at[z], {"ctx": to, "exp": e}
            ).start()

    x_sends = []
    for k in (2, 1, 3):
        _, device = x_peer(k)
        x_sends.append(send(qd.at[x], qd.at[x], x_ss.at[k], x_rs.at[x], device))
        x_sends[-1].start()

    @pl.loop(1, NE)
    def _(k):
        to = lax.rem(e + k, NE)
        send(
            outgoing.at[pl.ds(pl.multiple_of(to * MSG, MSG), MSG)],
            incoming.at[pl.ds(pl.multiple_of(e * MSG, MSG), MSG)],
            a_ss,
            a_rs,
            {"ctx": z, "exp": to},
        ).start()

    own_rows = pl.ds(pl.multiple_of(e * MSG, MSG), MSG)
    own_tokens = pltpu.make_async_copy(outgoing.at[own_rows], incoming.at[own_rows], loc.at[0])
    own_tokens.start()

    @pl.loop(0, NZ)
    def _(j):
        @pl.when(j < z)
        def _():
            send(kv.at[c, j], kv.at[c, j], kv_ss.at[j], kv_rs.at[j], partner).wait_recv()

    swap = send(kv.at[c], kv.at[c], c_ss.at[0], c_rs.at[0], partner)
    swap.start()
    for k in (1, 2, 3):
        other, device = x_peer(k)
        send(qd.at[other], qd.at[other], x_ss.at[k], x_rs.at[other], device).wait_recv()
    swap.wait_recv()

    keys = kv[0].reshape(KEYS, HEAD)
    values = kv[1].reshape(KEYS, HEAD)
    at = lax.broadcasted_iota(I32, (KEYS, ROWS), 0)
    key_pos = (at // SUB) * ROWS + x * SUB + lax.rem(at, SUB)
    query_pos = z * ROWS + lax.broadcasted_iota(I32, (KEYS, ROWS), 1)
    causal = key_pos <= query_pos
    stats[x, 12:16] = jnp.zeros((4, ROWS), F32)
    for h in range(NX):
        s = lax.dot_general(keys, qd[h, 0], contract_last, preferred_element_type=F32) * scale
        s = jnp.where(causal, s, MASKED)
        m = jnp.max(s, axis=0, keepdims=True)
        p = jnp.exp(s - m)
        d = lax.dot_general(values, qd[h, 1], contract_last, preferred_element_type=F32)
        pun[h] = p
        dps[h] = d
        stats[x, pl.ds(h, 1)] = m
        stats[x, pl.ds(4 + h, 1)] = jnp.sum(p, axis=0, keepdims=True)
        stats[x, pl.ds(8 + h, 1)] = jnp.sum(p * d, axis=0, keepdims=True)
    st_sends = []
    for k in (2, 1, 3):
        _, device = x_peer(k)
        st_sends.append(send(stats.at[x], stats.at[x], st_ss.at[k], st_rs.at[x], device))
        st_sends[-1].start()
    for k in (1, 2, 3):
        other, device = x_peer(k)
        send(stats.at[other], stats.at[other], st_ss.at[k], st_rs.at[other], device).wait_recv()

    highs = [stats[n, 0:4] for n in range(NX)]
    top = jnp.maximum(jnp.maximum(highs[0], highs[1]), jnp.maximum(highs[2], highs[3]))
    shifts = [jnp.exp(highs[n] - top) for n in range(NX)]
    mass = sum(stats[n, 4:8] * shifts[n] for n in range(NX))
    delta = sum(stats[n, 8:12] * shifts[n] for n in range(NX)) / mass
    factor = jnp.exp(stats[x, 0:4] - (top + jnp.log(mass)))

    keys_t = keys.astype(F32).T.astype(BF16)
    dk = jnp.zeros((KEYS, HEAD), F32)
    dv = jnp.zeros((KEYS, HEAD), F32)
    for h in range(NX):
        p = pun[h] * factor[h : h + 1]
        ds = (p * (dps[h] - delta[h : h + 1])).astype(BF16)
        dv += jnp.dot(p.astype(BF16), qd[h, 1], preferred_element_type=F32)
        dk += jnp.dot(ds, qd[h, 0], preferred_element_type=F32)
        dqs[h] = (jnp.dot(keys_t, ds, preferred_element_type=F32) * scale).astype(BF16)
    acc[:, 0:HEAD] = dk * scale
    acc[:, HEAD:] = dv
    grid = acc[...].reshape(NZ, 2, HALF, 2 * HEAD)
    for n in range(2):
        halves[n] = grid[:, n].astype(BF16)
    pair = send(halves.at[1 - c], core_in, c_ss.at[1], c_rs.at[1], partner)
    pair.start()
    dq_sends = []
    for k in (2, 1, 3):
        other, device = x_peer(k)
        dq_sends.append(send(dqs.at[other], dqr.at[x], dq_ss.at[k], dq_rs.at[x], device))
        dq_sends[-1].start()
    pair.wait_recv()
    zs[...] = (halves[c].astype(F32) + core_in[...].astype(F32)).astype(BF16)

    @pl.loop(0, NZ)
    def _(j):
        @pl.when(j < z)
        def _():
            send(zs.at[j], zr.at[z], z_ss.at[j], z_rs.at[z], {"ctx": j, "exp": e}).start()

    for copy in local[6:]:
        copy.wait()
    own_tokens.wait()
    most = pl.ds(0, (NE - 1) * MSG)
    pltpu.make_async_copy(incoming.at[most], incoming.at[most], a_rs).wait()
    hidden = jnp.zeros((SLOTS, FF), F32)
    slot = lax.broadcasted_iota(I32, (SLOTS, SLOTS * NQ), 0) * NQ
    place = lax.broadcasted_iota(I32, (SLOTS, SLOTS * NQ), 1)
    for n in range(NQ):
        take = jnp.where(place == slot + n, 1.0, 0.0).astype(BF16)
        part = jnp.dot(take, incoming[...], preferred_element_type=F32).astype(BF16)
        hidden += lax.dot_general(
            part, down_v[:, n * CH : (n + 1) * CH], contract_last, preferred_element_type=F32
        )
    gate = saved_v[:, :FF].astype(F32)
    up = saved_v[:, FF:].astype(F32)
    sig = 1.0 / (1.0 + jnp.exp(-gate))
    dgu_out[0, 0, :, :FF] = (hidden * up * sig * (1.0 + gate * (1.0 - sig))).astype(BF16)
    dgu_out[0, 0, :, FF:] = (hidden * gate * sig).astype(BF16)

    dq = dqs[x].astype(F32)
    for k in (1, 2, 3):
        other, device = x_peer(k)
        send(dqs.at[other], dqr.at[other], dq_ss.at[k], dq_rs.at[other], device).wait_recv()
        dq += dqr[other].astype(F32)
    dq_out[...] = dq.T.astype(BF16)

    @pl.loop(0, NZ)
    def _(j):
        @pl.when(j > z)
        def _():
            send(zs.at[j], zr.at[j], z_ss.at[j], z_rs.at[j], partner).wait_recv()

    summed = zs[z].astype(F32)
    for n in range(NZ):
        summed += zr[n].astype(F32)
    for n in range(8):
        fs[n] = summed[2 * n : 2 * n + 2]
    base = (2 * x + c) * 8
    for n in range(8):

        @pl.when(base + n != e)
        def _(n=n):
            send(fs.at[n], fr.at[y], f_ss.at[n], f_rs.at[y], {"ctx": z, "exp": base + n}).start()

        @pl.when(base + n == e)
        def _(n=n):
            fr[y] = fs[n]

    for n in range(NY):

        @pl.when(n * 8 + y != e)
        def _(n=n):
            send(fs.at[0], fr.at[n], f_ss.at[0], f_rs.at[n], partner).wait_recv()

    for n in range(4):
        dkv_out[:, n, :] = fr[2 * n] + fr[2 * n + 1]

    for copy in x_sends + st_sends + dq_sends + [swap, pair]:
        copy.wait_send()

    @pl.loop(0, NZ)
    def _(j):
        @pl.when(j > z)
        def _():
            send(kv.at[c, z], kv.at[c, z], kv_ss.at[j], kv_rs.at[j], partner).wait_send()

        @pl.when(j < z)
        def _():
            send(zs.at[j], zr.at[j], z_ss.at[j], z_rs.at[j], partner).wait_send()

    for n in range(8):

        @pl.when(base + n != e)
        def _(n=n):
            send(fs.at[n], fr.at[n], f_ss.at[n], f_rs.at[n], partner).wait_send()

    pltpu.make_async_copy(outgoing.at[most], outgoing.at[most], a_ss).wait()


def body(
    queries, keyvals, d_attn, grad_tokens, expert_ids, route_weights, saved_gate_up, down_weight
):
    dma = pltpu.SemaphoreType.DMA
    vmem = pltpu.VMEM
    return pl.pallas_call(
        kernel,
        out_shape=(
            jax.ShapeDtypeStruct((ROWS, HEAD), BF16),
            jax.ShapeDtypeStruct((2, 4, 2 * HEAD), F32),
            jax.ShapeDtypeStruct((1, 1, SLOTS, 2 * FF), BF16),
        ),
        in_specs=[pl.BlockSpec(memory_space=pltpu.HBM)] * 8,
        out_specs=tuple([pl.BlockSpec(memory_space=vmem)] * 3),
        scratch_shapes=[
            vmem((NX, 2, ROWS, HEAD), BF16),
            vmem((2, NZ, SUB, HEAD), BF16),
            vmem((NX, KEYS, ROWS), F32),
            vmem((NX, KEYS, ROWS), F32),
            vmem((NX, 16, ROWS), F32),
            vmem((NX, HEAD, ROWS), BF16),
            vmem((NX, HEAD, ROWS), BF16),
            vmem((KEYS, 2 * HEAD), F32),
            vmem((2, NZ, HALF, 2 * HEAD), BF16),
            vmem((NZ, HALF, 2 * HEAD), BF16),
            vmem((NZ, HALF, 2 * HEAD), BF16),
            vmem((NZ, HALF, 2 * HEAD), BF16),
            vmem((8, 2, 2 * HEAD), F32),
            vmem((NY, 2, 2 * HEAD), F32),
            vmem((8, NQ * CH), BF16),
            vmem((8, 8), I32),
            vmem((8, 8), F32),
            vmem((SLOTS, 2 * FF), BF16),
            vmem((FF, NQ * CH), BF16),
            vmem((SLOTS * NQ, CH), BF16),
            vmem((SLOTS * NQ, CH), BF16),
            dma((8,)),
            dma((NZ,)),
            dma((NZ,)),
            dma((4,)),
            dma((4,)),
            dma((4,)),
            dma((4,)),
            dma((4,)),
            dma((4,)),
            dma((2,)),
            dma((2,)),
            dma((NZ,)),
            dma((NZ,)),
            dma((8,)),
            dma((8,)),
            dma,
            dma,
        ],
        compiler_params=pltpu.CompilerParams(
            collective_id=0, has_side_effects=True, vmem_limit_bytes=60 * 1024 * 1024
        ),
        name="layer_backward",
    )(
        queries, keyvals, d_attn, grad_tokens, expert_ids, route_weights, saved_gate_up, down_weight
    )


def solution(mesh):
    placed = (
        P("ctx", "exp"),
        P(None, "ctx", None),
        P("ctx", "exp"),
        P(("ctx", "exp"), None),
        P(("ctx", "exp"), None),
        P(("ctx", "exp"), None),
        P("ctx", "exp", None, None),
        P("exp", None, None),
    )
    return jax.shard_map(
        body,
        mesh=mesh,
        in_specs=placed,
        out_specs=(P("ctx", "exp"), P(("ctx", "exp"), None, None), P("ctx", "exp", None, None)),
        check_vma=False,
    )
```

```python
import math

import jax
import jax.numpy as jnp
from jax import lax
from jax.experimental import pallas as pl
from jax.experimental.pallas import tpu as pltpu
from jax.sharding import PartitionSpec as P

MESH = pl.DeviceIdType.MESH
F32, BF16, I32 = jnp.float32, jnp.bfloat16, jnp.int32

NZ = 16
NP = 8
ROWS = 128
HEAD = 128
SUB = ROWS // NP
KEYS = NZ * SUB
QUERIES = NP * ROWS
FF = 768
WIDTH = 4096
SIDE = WIDTH // 2
EXTRA = 128
CUT = SIDE // 2
SLOTS = 128
MASKED = -1e30

contract_last = (((1,), (1,)), ((), ()))


def send(src, dst, ss, rs, device):
    return pltpu.make_async_remote_copy(
        src_ref=src, dst_ref=dst, send_sem=ss, recv_sem=rs, device_id=device, device_id_type=MESH
    )


def choices(ids, weights):
    ids = ids.astype(F32)
    token = lax.broadcasted_iota(I32, (8, 8), 0)
    slot = jnp.zeros((8, 8), F32)
    for t in range(7):
        for k in range(8):
            slot += jnp.where((ids[t : t + 1, k : k + 1] == ids) & (token > t), 1.0, 0.0)
    high = weights.astype(BF16)
    low = (weights - high.astype(F32)).astype(BF16)
    at = lax.broadcasted_iota(I32, (8, EXTRA), 1) - lax.broadcasted_iota(I32, (8, EXTRA), 0)
    out = jnp.zeros((8, EXTRA), F32)
    for n, part in enumerate(((ids * 2.0 + slot).astype(BF16), high, low)):
        spread = jnp.where(at == 8 * n, 1.0, 0.0).astype(BF16)
        out += jnp.dot(part, spread, preferred_element_type=F32)
    return out


def kernel(
    q_ref, kv_ref, do_ref, tok_ref, ids_ref, wts_ref, saved_ref, down_ref,
    dq_out, dkv_out, dgu_out,
    block, kv, qd, pun, dps, pb, sb, stats, dqs, dqr, zs, zr, fs, fr,
    tok_v, ids_v, wts_v, saved_v, down_v, tb, outgoing, incoming,
    loc, kv_ss, kv_rs, x_ss, x_rs, st_ss, st_rs, dq_ss, dq_rs,
    z_ss, z_rs, f_ss, f_rs, t_ss, t_rs, a_ss, a_rs,
):
    z, e = lax.axis_index("ctx"), lax.axis_index("exp")
    d = lax.rem(e, NP)
    y = e // NP
    g = y // 2
    scale = 1.0 / math.sqrt(HEAD)

    def row(k):
        other = lax.rem(d + k, NP)
        return other, {"ctx": z, "exp": y * NP + other}

    def column(k):
        other = lax.rem(y + k, NP)
        return other, {"ctx": z, "exp": other * NP + d}

    partner = {"ctx": z, "exp": e + 1 - 2 * lax.rem(e, 2)}
    order = (4, 5, 3, 2, 6, 7, 1)
    cuts = (pl.ds(0, EXTRA + CUT), pl.ds(EXTRA + CUT, CUT))
    own = pl.ds(pl.multiple_of(d * 16, 16), 16)

    local = [
        pltpu.make_async_copy(kv_ref.at[:, :, pl.ds(g * HEAD, HEAD)], block, loc.at[0]),
        pltpu.make_async_copy(q_ref, qd.at[0, d], loc.at[1]),
        pltpu.make_async_copy(do_ref, qd.at[1, d], loc.at[2]),
        pltpu.make_async_copy(tok_ref, tok_v, loc.at[3]),
        pltpu.make_async_copy(ids_ref, ids_v, loc.at[4]),
        pltpu.make_async_copy(wts_ref, wts_v, loc.at[5]),
        pltpu.make_async_copy(saved_ref.at[0, 0], saved_v, loc.at[6]),
        pltpu.make_async_copy(down_ref.at[0], down_v, loc.at[7]),
    ]
    for copy in local:
        copy.start()

    kv[...] = jnp.zeros_like(kv)
    zr[...] = jnp.zeros_like(zr)
    barrier = pltpu.get_barrier_semaphore()

    @pl.loop(1, NZ)
    def _(k):
        pl.semaphore_signal(
            barrier, inc=1, device_id={"ctx": lax.rem(z + k, NZ), "exp": e}, device_id_type=MESH
        )

    for k in range(1, NP):
        for _, device in (row(k), column(k)):
            pl.semaphore_signal(barrier, inc=1, device_id=device, device_id_type=MESH)

    local[0].wait()
    near = lax.broadcasted_iota(I32, (SUB, ROWS), 0)
    far = lax.broadcasted_iota(I32, (SUB, ROWS), 1)
    chosen = (far == (near // 2) * SUB + 2 * d + lax.rem(near, 2)).astype(F32).astype(BF16)
    for n in range(2):
        kv[z, n] = jnp.dot(chosen, block[n], preferred_element_type=F32).astype(BF16)

    for copy in local[3:6]:
        copy.wait()
    wide = tok_v[...].astype(F32)
    tb[y, :, EXTRA:] = jnp.concatenate([wide[:, :SIDE], wide[:, SIDE:]], axis=0).astype(BF16)
    beside = choices(ids_v[...], wts_v[...])
    tb[y, :, :EXTRA] = jnp.concatenate([beside, beside], axis=0).astype(BF16)
    for copy in local[1:3]:
        copy.wait()

    pl.semaphore_wait(barrier, NZ - 1 + 2 * (NP - 1))

    @pl.loop(1, NZ)
    def _(k):
        to = NZ - k

        @pl.when(to > z)
        def _():
            send(kv.at[z], kv.at[z], kv_ss.at[to], kv_rs.at[z], {"ctx": to, "exp": e}).start()

    sends = []

    def start(copy):
        copy.start()
        sends.append(copy)

    for k in order:
        _, device = row(k)
        start(send(qd.at[:, d], qd.at[:, d], x_ss.at[k], x_rs.at[d], device))
    for n, cut in enumerate(cuts):
        for k in order:
            _, device = column(k)
            mine = tb.at[y, :, cut]
            start(send(mine, mine, t_ss.at[n, k], t_rs.at[n, y], device))

    for k in range(1, NP):
        other, _ = row(k)
        send(qd.at[:, other], qd.at[:, other], x_ss.at[k], x_rs.at[other], partner).wait_recv()

    @pl.loop(0, NZ)
    def _(j):
        @pl.when(j < z)
        def _():
            send(kv.at[j], kv.at[j], kv_ss.at[j], kv_rs.at[j], partner).wait_recv()

    keys = kv[:, 0].reshape(KEYS, HEAD)
    values = kv[:, 1].reshape(KEYS, HEAD)
    at = lax.broadcasted_iota(I32, (KEYS, ROWS), 0)
    in_block = lax.rem(at, SUB)
    key_pos = (at // SUB) * ROWS + (in_block // 2) * SUB + 2 * d + lax.rem(in_block, 2)
    causal = key_pos <= z * ROWS + lax.broadcasted_iota(I32, (KEYS, ROWS), 1)
    for h in range(NP):
        s = lax.dot_general(keys, qd[0, h], contract_last, preferred_element_type=F32) * scale
        s = jnp.where(causal, s, MASKED)
        m = jnp.max(s, axis=0, keepdims=True)
        p = jnp.exp(s - m)
        v = lax.dot_general(values, qd[1, h], contract_last, preferred_element_type=F32)
        pun[h] = p
        dps[h] = v
        stats[d, pl.ds(h, 1)] = m
        stats[d, pl.ds(NP + h, 1)] = jnp.sum(p, axis=0, keepdims=True)
        stats[d, pl.ds(2 * NP + h, 1)] = jnp.sum(p * v, axis=0, keepdims=True)
    for k in order:
        _, device = row(k)
        start(send(stats.at[d], stats.at[d], st_ss.at[k], st_rs.at[d], device))

    def await_tokens(n):
        for k in range(1, NP):
            other, _ = column(k)
            theirs = tb.at[other, :, cuts[n]]
            send(theirs, theirs, t_ss.at[n, k], t_rs.at[n, other], partner).wait_recv()

    await_tokens(0)
    beside = tb[:, :, :EXTRA].reshape(SLOTS, EXTRA).astype(F32).T
    r = lax.broadcasted_iota(I32, (SLOTS, SLOTS), 0)
    q = lax.broadcasted_iota(I32, (SLOTS, SLOTS), 1)
    wanted = ((y * NP + r // 16) * 2 + lax.rem(r, 2)).astype(F32)
    same = lax.rem(r, 16) // 2 == q // 16
    high = jnp.zeros((SLOTS, SLOTS), F32)
    low = jnp.zeros((SLOTS, SLOTS), F32)
    for k in range(8):
        hit = same & (beside[k : k + 1] == wanted)
        high += jnp.where(hit, beside[8 + k : 9 + k], 0.0)
        low += jnp.where(hit, beside[16 + k : 17 + k], 0.0)
    first = lax.rem(q, 16) < 8
    placers = [
        [jnp.where(first, part, 0.0).astype(BF16), jnp.where(first, 0.0, part).astype(BF16)]
        for part in (high, low)
    ]

    def pack(n):
        for half in range(2):
            for m in range(2):
                at = EXTRA + n * CUT + m * 512
                part = tb[:, :, at : at + 512].reshape(SLOTS, 512)
                outgoing[n, :, half * CUT + m * 512 : half * CUT + (m + 1) * 512] = (
                    jnp.dot(placers[0][half], part, preferred_element_type=F32)
                    + jnp.dot(placers[1][half], part, preferred_element_type=F32)
                ).astype(BF16)
        for k in order:
            other, device = row(k)
            theirs = pl.ds(pl.multiple_of(other * 16, 16), 16)
            start(
                send(
                    outgoing.at[n, theirs], incoming.at[n, own], a_ss.at[n, k], a_rs.at[n, d], device
                )
            )
        keep = pltpu.make_async_copy(outgoing.at[n, own], incoming.at[n, own], loc.at[n])
        keep.start()
        return keep

    own_tokens = [pack(0)]

    for k in range(1, NP):
        other, _ = row(k)
        send(stats.at[other], stats.at[other], st_ss.at[k], st_rs.at[other], partner).wait_recv()

    top = stats[0, 0:NP]
    for n in range(1, NP):
        top = jnp.maximum(top, stats[n, 0:NP])
    shifts = [jnp.exp(stats[n, 0:NP] - top) for n in range(NP)]
    mass = sum(stats[n, NP : 2 * NP] * shifts[n] for n in range(NP))
    delta = sum(stats[n, 2 * NP : 3 * NP] * shifts[n] for n in range(NP)) / mass
    factor = jnp.exp(stats[d, 0:NP] - (top + jnp.log(mass)))
    for h in range(NP):
        p = pun[h] * factor[h : h + 1]
        pb[:, h * ROWS : (h + 1) * ROWS] = p.astype(BF16)
        sb[:, h * ROWS : (h + 1) * ROWS] = (p * (dps[h] - delta[h : h + 1])).astype(BF16)
    dk = jnp.dot(sb[...], qd[0].reshape(QUERIES, HEAD), preferred_element_type=F32) * scale
    zs[:, :, :HEAD] = dk.astype(BF16).reshape(NZ, SUB, HEAD)
    dv = jnp.dot(pb[...], qd[1].reshape(QUERIES, HEAD), preferred_element_type=F32)
    zs[:, :, HEAD:] = dv.astype(BF16).reshape(NZ, SUB, HEAD)

    @pl.loop(0, NZ)
    def _(j):
        @pl.when(j < z)
        def _():
            send(zs.at[j], zr.at[z], z_ss.at[j], z_rs.at[z], {"ctx": j, "exp": e}).start()

    await_tokens(1)
    own_tokens.append(pack(1))

    keys_t = keys.astype(F32).T.astype(BF16)
    for h in range(NP):
        dqs[h] = (
            jnp.dot(keys_t, sb[:, h * ROWS : (h + 1) * ROWS], preferred_element_type=F32) * scale
        ).astype(BF16)
    for k in order:
        other, device = row(k)
        start(send(dqs.at[other], dqr.at[d], dq_ss.at[k], dq_rs.at[d], device))

    for copy in local[6:]:
        copy.wait()
    swap = (lax.rem(r, 16) // 2 == q // 16) & (r // 16 == lax.rem(q, 16) // 2)
    swap = (swap & (lax.rem(r, 2) == lax.rem(q, 2))).astype(F32).astype(BF16)

    def down_part(n):
        own_tokens[n].wait()
        for k in range(1, NP):
            other, _ = row(k)
            theirs = pl.ds(pl.multiple_of(other * 16, 16), 16)
            send(
                outgoing.at[n, own], incoming.at[n, theirs], a_ss.at[n, k], a_rs.at[n, other], partner
            ).wait_recv()
        total = jnp.zeros((SLOTS, FF), F32)
        for half in range(2):
            part = incoming[n, :, half * CUT : (half + 1) * CUT]
            rows = jnp.dot(swap, part, preferred_element_type=F32).astype(BF16)
            at = half * SIDE + n * CUT
            total += lax.dot_general(
                rows, down_v[:, at : at + CUT], contract_last, preferred_element_type=F32
            )
        return total

    hidden = down_part(0)

    @pl.loop(0, NZ)
    def _(j):
        @pl.when(j > z)
        def _():
            send(zs.at[j], zr.at[j], z_ss.at[j], z_rs.at[j], partner).wait_recv()

    summed = zs[z].astype(F32)
    for n in range(NZ):
        summed += zr[n].astype(F32)
    for n in range(NP):
        fs[n] = summed[2 * n : 2 * n + 2]
    fr[y] = fs[y]
    for k in range(1, NP):
        other, device = column(k)
        start(send(fs.at[other], fr.at[y], f_ss.at[k], f_rs.at[y], device))

    dq = dqs[d].astype(F32)
    for k in range(1, NP):
        other, _ = row(k)
        send(dqs.at[other], dqr.at[other], dq_ss.at[k], dq_rs.at[other], partner).wait_recv()
        dq += dqr[other].astype(F32)
    dq_out[...] = dq.T.astype(BF16)

    hidden += down_part(1)
    gate = saved_v[:, :FF].astype(F32)
    up = saved_v[:, FF:].astype(F32)
    sig = 1.0 / (1.0 + jnp.exp(-gate))
    dgu_out[0, 0, :, :FF] = (hidden * up * sig * (1.0 + gate * (1.0 - sig))).astype(BF16)
    dgu_out[0, 0, :, FF:] = (hidden * gate * sig).astype(BF16)

    for k in range(1, NP):
        other, _ = column(k)
        send(fs.at[other], fr.at[other], f_ss.at[k], f_rs.at[other], partner).wait_recv()
    for n in range(4):
        dkv_out[:, n, :] = fr[2 * n] + fr[2 * n + 1]

    for copy in sends:
        copy.wait_send()

    @pl.loop(0, NZ)
    def _(j):
        @pl.when(j > z)
        def _():
            send(kv.at[z], kv.at[z], kv_ss.at[j], kv_rs.at[j], partner).wait_send()

        @pl.when(j < z)
        def _():
            send(zs.at[j], zr.at[j], z_ss.at[j], z_rs.at[j], partner).wait_send()


def store_kernel(a_ref, b_ref, c_ref, a_out, b_out, c_out, sems):
    copies = [
        pltpu.make_async_copy(src, dst, sems.at[n])
        for n, (src, dst) in enumerate(((c_ref, c_out), (a_ref, a_out), (b_ref, b_out)))
    ]
    for copy in copies:
        copy.start()
    for copy in copies:
        copy.wait()


def body(
    queries, keyvals, d_attn, grad_tokens, expert_ids, route_weights, saved_gate_up, down_weight
):
    dma = pltpu.SemaphoreType.DMA
    vmem = pltpu.VMEM
    shapes = (
        jax.ShapeDtypeStruct((ROWS, HEAD), BF16),
        jax.ShapeDtypeStruct((2, 4, 2 * HEAD), F32),
        jax.ShapeDtypeStruct((1, 1, SLOTS, 2 * FF), BF16),
    )
    outs = pl.pallas_call(
        kernel,
        out_shape=shapes,
        in_specs=[pl.BlockSpec(memory_space=pl.ANY)] * 8,
        out_specs=tuple([pl.BlockSpec(memory_space=vmem)] * 3),
        scratch_shapes=[
            vmem((2, ROWS, HEAD), BF16),
            vmem((NZ, 2, SUB, HEAD), BF16),
            vmem((2, NP, ROWS, HEAD), BF16),
            vmem((NP, KEYS, ROWS), F32),
            vmem((NP, KEYS, ROWS), F32),
            vmem((KEYS, QUERIES), BF16),
            vmem((KEYS, QUERIES), BF16),
            vmem((NP, 3 * NP, ROWS), F32),
            vmem((NP, HEAD, ROWS), BF16),
            vmem((NP, HEAD, ROWS), BF16),
            vmem((NZ, SUB, 2 * HEAD), BF16),
            vmem((NZ, SUB, 2 * HEAD), BF16),
            vmem((NP, 2, 2 * HEAD), F32),
            vmem((NP, 2, 2 * HEAD), F32),
            vmem((8, WIDTH), BF16),
            vmem((8, 8), I32),
            vmem((8, 8), F32),
            vmem((SLOTS, 2 * FF), BF16),
            vmem((FF, WIDTH), BF16),
            vmem((NP, 16, SIDE + EXTRA), BF16),
            vmem((2, SLOTS, SIDE), BF16),
            vmem((2, SLOTS, SIDE), BF16),
            dma((8,)),
        ]
        + [dma((n,)) for n in (NZ, NZ, NP, NP, NP, NP, NP, NP, NZ, NZ, NP, NP)]
        + [dma((2, NP))] * 4,
        compiler_params=pltpu.CompilerParams(
            collective_id=0, has_side_effects=True, vmem_limit_bytes=60 * 1024 * 1024
        ),
        name="layer_backward",
    )(
        queries, keyvals, d_attn, grad_tokens, expert_ids, route_weights, saved_gate_up, down_weight
    )
    return pl.pallas_call(
        store_kernel,
        out_shape=shapes,
        in_specs=[pl.BlockSpec(memory_space=vmem)] * 3,
        out_specs=tuple([pl.BlockSpec(memory_space=pl.ANY)] * 3),
        scratch_shapes=[dma((3,))],
        name="store",
    )(*outs)


def solution(mesh):
    placed = (
        P("ctx", "exp"),
        P(None, "ctx", None),
        P("ctx", "exp"),
        P(("ctx", "exp"), None),
        P(("ctx", "exp"), None),
        P(("ctx", "exp"), None),
        P("ctx", "exp", None, None),
        P("exp", None, None),
    )
    return jax.shard_map(
        body,
        mesh=mesh,
        in_specs=placed,
        out_specs=(P("ctx", "exp"), P(("ctx", "exp"), None, None), P("ctx", "exp", None, None)),
        check_vma=False,
    )
```

```python
import math

import jax
import jax.numpy as jnp
from jax import lax
from jax.experimental import pallas as pl
from jax.experimental.pallas import tpu as pltpu
from jax.sharding import PartitionSpec as P

MESH = pl.DeviceIdType.MESH
F32, BF16, I32 = jnp.float32, jnp.bfloat16, jnp.int32

NZ = 16
NP = 8
ROWS = 128
HEAD = 128
SUB = ROWS // NP
KEYS = NZ * SUB
QUERIES = NP * ROWS
FF = 768
WIDTH = 4096
SIDE = WIDTH // 2
EXTRA = 128
CUT = SIDE // 2
SLOTS = 128
MASKED = -1e30
LATE = 8

contract_last = (((1,), (1,)), ((), ()))


def send(src, dst, ss, rs, device):
    return pltpu.make_async_remote_copy(
        src_ref=src, dst_ref=dst, send_sem=ss, recv_sem=rs, device_id=device, device_id_type=MESH
    )


def choices(ids, weights):
    ids = ids.astype(F32)
    token = lax.broadcasted_iota(I32, (8, 8), 0)
    slot = jnp.zeros((8, 8), F32)
    for t in range(7):
        for k in range(8):
            slot += jnp.where((ids[t : t + 1, k : k + 1] == ids) & (token > t), 1.0, 0.0)
    high = weights.astype(BF16)
    low = (weights - high.astype(F32)).astype(BF16)
    at = lax.broadcasted_iota(I32, (8, EXTRA), 1) - lax.broadcasted_iota(I32, (8, EXTRA), 0)
    out = jnp.zeros((8, EXTRA), F32)
    for n, part in enumerate(((ids * 2.0 + slot).astype(BF16), high, low)):
        spread = jnp.where(at == 8 * n, 1.0, 0.0).astype(BF16)
        out += jnp.dot(part, spread, preferred_element_type=F32)
    return out


def kernel(
    q_ref, kv_ref, do_ref, tok_ref, ids_ref, wts_ref, saved_ref, down_ref,
    dq_hbm, dkv_hbm, dgu_hbm,
    dq_out, dkv_out, dgu_out, block, kv, qd, pun, dps, pb, sb, stats, dqs, dqr, zs, zr, fs, fr,
    tok_v, ids_v, wts_v, saved_v, down_v, tb, placers, outgoing, incoming,
    loc, kv_ss, kv_rs, x_ss, x_rs, st_ss, st_rs, dq_ss, dq_rs,
    z_ss, z_rs, f_ss, f_rs, t_ss, t_rs, a_ss, a_rs,
):
    z, e = lax.axis_index("ctx"), lax.axis_index("exp")
    d = lax.rem(e, NP)
    y = e // NP
    g = y // 2
    scale = 1.0 / math.sqrt(HEAD)

    def row(k):
        other = lax.rem(d + k, NP)
        return other, {"ctx": z, "exp": y * NP + other}

    def column(k):
        other = lax.rem(y + k, NP)
        return other, {"ctx": z, "exp": other * NP + d}

    partner = {"ctx": z, "exp": e + 1 - 2 * lax.rem(e, 2)}
    order = (4, 5, 3, 2, 6, 7, 1)
    cuts = (pl.ds(0, EXTRA + CUT), pl.ds(EXTRA + CUT, CUT))
    own = pl.ds(pl.multiple_of(d * 16, 16), 16)

    kv[...] = jnp.zeros_like(kv)
    zr[...] = jnp.zeros_like(zr)
    barrier = pltpu.get_barrier_semaphore()

    @pl.loop(0, NZ - 1)
    def _(k):
        at = lax.rem(z + 8 + k + k // 8, NZ)
        pl.semaphore_signal(barrier, inc=1, device_id={"ctx": at, "exp": e}, device_id_type=MESH)

    for k in range(1, NP):
        for _, device in (row(k), column(k)):
            pl.semaphore_signal(barrier, inc=1, device_id=device, device_id_type=MESH)

    local = [
        pltpu.make_async_copy(kv_ref.at[:, :, pl.ds(g * HEAD, HEAD)], block, loc.at[0]),
        pltpu.make_async_copy(q_ref, qd.at[0, d], loc.at[1]),
        pltpu.make_async_copy(do_ref, qd.at[1, d], loc.at[2]),
        pltpu.make_async_copy(tok_ref, tok_v, loc.at[3]),
        pltpu.make_async_copy(ids_ref, ids_v, loc.at[4]),
        pltpu.make_async_copy(wts_ref, wts_v, loc.at[5]),
        pltpu.make_async_copy(saved_ref.at[0, 0], saved_v, loc.at[6]),
        pltpu.make_async_copy(down_ref.at[0], down_v, loc.at[7]),
    ]
    for copy in local:
        copy.start()

    local[0].wait()
    near = lax.broadcasted_iota(I32, (SUB, ROWS), 0)
    far = lax.broadcasted_iota(I32, (SUB, ROWS), 1)
    chosen = (far == (near // 2) * SUB + 2 * d + lax.rem(near, 2)).astype(F32).astype(BF16)
    for n in range(2):
        kv[z, n] = jnp.dot(chosen, block[n], preferred_element_type=F32).astype(BF16)

    for copy in local[3:6]:
        copy.wait()
    wide = tok_v[...].astype(F32)
    tb[y, :, EXTRA:] = jnp.concatenate([wide[:, :SIDE], wide[:, SIDE:]], axis=0).astype(BF16)
    beside = choices(ids_v[...], wts_v[...])
    tb[y, :, :EXTRA] = jnp.concatenate([beside, beside], axis=0).astype(BF16)
    for copy in local[1:3]:
        copy.wait()

    pl.semaphore_wait(barrier, NZ - 1 + 2 * (NP - 1))

    @pl.loop(1, NZ)
    def _(k):
        to = z + jnp.where(k <= 8, 9 - k, k)

        @pl.when(to < NZ)
        def _():
            send(kv.at[z], kv.at[z], kv_ss.at[to], kv_rs.at[z], {"ctx": to, "exp": e}).start()

    sends = []

    def start(copy):
        copy.start()
        sends.append(copy)

    for k in order:
        _, device = row(k)
        start(send(qd.at[:, d], qd.at[:, d], x_ss.at[k], x_rs.at[d], device))
    def send_tokens():
        for n, cut in enumerate(cuts):
            for k in order:
                _, device = column(k)
                mine = tb.at[y, :, cut]
                send(mine, mine, t_ss.at[n, k], t_rs.at[n, y], device).start()

    late = z >= LATE
    pl.when(jnp.logical_not(late))(send_tokens)

    for k in range(1, NP):
        other, _ = row(k)
        send(qd.at[:, other], qd.at[:, other], x_ss.at[k], x_rs.at[other], partner).wait_recv()

    @pl.loop(0, NZ)
    def _(j):
        @pl.when(j < z)
        def _():
            send(kv.at[j], kv.at[j], kv_ss.at[j], kv_rs.at[j], partner).wait_recv()

    keys = kv[:, 0].reshape(KEYS, HEAD)
    values = kv[:, 1].reshape(KEYS, HEAD)
    at = lax.broadcasted_iota(I32, (KEYS, ROWS), 0)
    in_block = lax.rem(at, SUB)
    key_pos = (at // SUB) * ROWS + (in_block // 2) * SUB + 2 * d + lax.rem(in_block, 2)
    causal = key_pos <= z * ROWS + lax.broadcasted_iota(I32, (KEYS, ROWS), 1)
    for h in range(NP):
        s = lax.dot_general(keys, qd[0, h], contract_last, preferred_element_type=F32) * scale
        s = jnp.where(causal, s, MASKED)
        m = jnp.max(s, axis=0, keepdims=True)
        p = jnp.exp(s - m)
        v = lax.dot_general(values, qd[1, h], contract_last, preferred_element_type=F32)
        pun[h] = p
        dps[h] = v
        stats[d, pl.ds(h, 1)] = m
        stats[d, pl.ds(NP + h, 1)] = jnp.sum(p, axis=0, keepdims=True)
        stats[d, pl.ds(2 * NP + h, 1)] = jnp.sum(p * v, axis=0, keepdims=True)
    for k in order:
        _, device = row(k)
        start(send(stats.at[d], stats.at[d], st_ss.at[k], st_rs.at[d], device))

    def await_tokens(n):
        for k in range(1, NP):
            other, _ = column(k)
            theirs = tb.at[other, :, cuts[n]]
            send(theirs, theirs, t_ss.at[n, k], t_rs.at[n, other], partner).wait_recv()

    r = lax.broadcasted_iota(I32, (SLOTS, SLOTS), 0)
    q = lax.broadcasted_iota(I32, (SLOTS, SLOTS), 1)

    def pack(n):
        for half in range(2):
            for m in range(2):
                at = EXTRA + n * CUT + m * 512
                part = tb[:, :, at : at + 512].reshape(SLOTS, 512)
                outgoing[n, :, half * CUT + m * 512 : half * CUT + (m + 1) * 512] = (
                    jnp.dot(placers[0, half], part, preferred_element_type=F32)
                    + jnp.dot(placers[1, half], part, preferred_element_type=F32)
                ).astype(BF16)
        for k in order:
            other, device = row(k)
            theirs = pl.ds(pl.multiple_of(other * 16, 16), 16)
            (
                send(
                    outgoing.at[n, theirs], incoming.at[n, own], a_ss.at[n, k], a_rs.at[n, d], device
                )
            ).start()
        pltpu.make_async_copy(outgoing.at[n, own], incoming.at[n, own], loc.at[n]).start()

    def first_part():
        await_tokens(0)
        beside = tb[:, :, :EXTRA].reshape(SLOTS, EXTRA).astype(F32).T
        wanted = ((y * NP + r // 16) * 2 + lax.rem(r, 2)).astype(F32)
        same = lax.rem(r, 16) // 2 == q // 16
        high = jnp.zeros((SLOTS, SLOTS), F32)
        low = jnp.zeros((SLOTS, SLOTS), F32)
        for k in range(8):
            hit = same & (beside[k : k + 1] == wanted)
            high += jnp.where(hit, beside[8 + k : 9 + k], 0.0)
            low += jnp.where(hit, beside[16 + k : 17 + k], 0.0)
        first = lax.rem(q, 16) < 8
        for n, part in enumerate((high, low)):
            placers[n, 0] = jnp.where(first, part, 0.0).astype(BF16)
            placers[n, 1] = jnp.where(first, 0.0, part).astype(BF16)
        pack(0)

    pl.when(jnp.logical_not(late))(first_part)

    for k in range(1, NP):
        other, _ = row(k)
        send(stats.at[other], stats.at[other], st_ss.at[k], st_rs.at[other], partner).wait_recv()

    top = stats[0, 0:NP]
    for n in range(1, NP):
        top = jnp.maximum(top, stats[n, 0:NP])
    shifts = [jnp.exp(stats[n, 0:NP] - top) for n in range(NP)]
    mass = sum(stats[n, NP : 2 * NP] * shifts[n] for n in range(NP))
    delta = sum(stats[n, 2 * NP : 3 * NP] * shifts[n] for n in range(NP)) / mass
    factor = jnp.exp(stats[d, 0:NP] - (top + jnp.log(mass)))
    for h in range(NP):
        p = pun[h] * factor[h : h + 1]
        pb[:, h * ROWS : (h + 1) * ROWS] = p.astype(BF16)
        sb[:, h * ROWS : (h + 1) * ROWS] = (p * (dps[h] - delta[h : h + 1])).astype(BF16)
    dk = jnp.dot(sb[...], qd[0].reshape(QUERIES, HEAD), preferred_element_type=F32) * scale
    zs[:, :, :HEAD] = dk.astype(BF16).reshape(NZ, SUB, HEAD)
    dv = jnp.dot(pb[...], qd[1].reshape(QUERIES, HEAD), preferred_element_type=F32)
    zs[:, :, HEAD:] = dv.astype(BF16).reshape(NZ, SUB, HEAD)

    @pl.loop(0, NZ)
    def _(j):
        @pl.when(j < z)
        def _():
            send(zs.at[j], zr.at[z], z_ss.at[j], z_rs.at[z], {"ctx": j, "exp": e}).start()

    pl.when(late)(send_tokens)

    keys_t = keys.astype(F32).T.astype(BF16)
    for h in range(NP):
        dqs[h] = (
            jnp.dot(keys_t, sb[:, h * ROWS : (h + 1) * ROWS], preferred_element_type=F32) * scale
        ).astype(BF16)
    for k in order:
        other, device = row(k)
        start(send(dqs.at[other], dqr.at[d], dq_ss.at[k], dq_rs.at[d], device))

    pl.when(late)(first_part)
    await_tokens(1)
    pack(1)

    for copy in local[6:]:
        copy.wait()
    swap = (lax.rem(r, 16) // 2 == q // 16) & (r // 16 == lax.rem(q, 16) // 2)
    swap = (swap & (lax.rem(r, 2) == lax.rem(q, 2))).astype(F32).astype(BF16)

    def down_part(n):
        pltpu.make_async_copy(outgoing.at[n, own], incoming.at[n, own], loc.at[n]).wait()
        for k in range(1, NP):
            other, _ = row(k)
            theirs = pl.ds(pl.multiple_of(other * 16, 16), 16)
            send(
                outgoing.at[n, own], incoming.at[n, theirs], a_ss.at[n, k], a_rs.at[n, other], partner
            ).wait_recv()
        total = jnp.zeros((SLOTS, FF), F32)
        for half in range(2):
            part = incoming[n, :, half * CUT : (half + 1) * CUT]
            rows = jnp.dot(swap, part, preferred_element_type=F32).astype(BF16)
            at = half * SIDE + n * CUT
            total += lax.dot_general(
                rows, down_v[:, at : at + CUT], contract_last, preferred_element_type=F32
            )
        return total

    hidden = down_part(0)

    @pl.loop(0, NZ)
    def _(j):
        @pl.when(j > z)
        def _():
            send(zs.at[j], zr.at[j], z_ss.at[j], z_rs.at[j], partner).wait_recv()

    summed = zs[z].astype(F32)
    for n in range(NZ):
        summed += zr[n].astype(F32)
    for n in range(NP):
        fs[n] = summed[2 * n : 2 * n + 2]
    fr[y] = fs[y]
    for k in range(1, NP):
        other, device = column(k)
        start(send(fs.at[other], fr.at[y], f_ss.at[k], f_rs.at[y], device))

    dq = dqs[d].astype(F32)
    for k in range(1, NP):
        other, _ = row(k)
        send(dqs.at[other], dqr.at[other], dq_ss.at[k], dq_rs.at[other], partner).wait_recv()
        dq += dqr[other].astype(F32)
    dq_out[...] = dq.T.astype(BF16)
    written = [pltpu.make_async_copy(dq_out, dq_hbm, loc.at[2])]
    written[-1].start()

    hidden += down_part(1)
    gate = saved_v[:, :FF].astype(F32)
    up = saved_v[:, FF:].astype(F32)
    sig = 1.0 / (1.0 + jnp.exp(-gate))
    dgu_out[:, :FF] = (hidden * up * sig * (1.0 + gate * (1.0 - sig))).astype(BF16)
    dgu_out[:, FF:] = (hidden * gate * sig).astype(BF16)
    written.append(pltpu.make_async_copy(dgu_out, dgu_hbm.at[0, 0], loc.at[3]))
    written[-1].start()

    for k in range(1, NP):
        other, _ = column(k)
        send(fs.at[other], fr.at[other], f_ss.at[k], f_rs.at[other], partner).wait_recv()
    for n in range(4):
        dkv_out[:, n, :] = fr[2 * n] + fr[2 * n + 1]
    written.append(pltpu.make_async_copy(dkv_out, dkv_hbm, loc.at[4]))
    written[-1].start()

    for copy in sends:
        copy.wait_send()
    for n, cut in enumerate(cuts):
        for k in order:
            mine = tb.at[y, :, cut]
            send(mine, mine, t_ss.at[n, k], t_rs.at[n, y], partner).wait_send()
            send(
                outgoing.at[n, own], incoming.at[n, own], a_ss.at[n, k], a_rs.at[n, d], partner
            ).wait_send()
    for copy in written:
        copy.wait()

    @pl.loop(0, NZ)
    def _(j):
        @pl.when(j > z)
        def _():
            send(kv.at[z], kv.at[z], kv_ss.at[j], kv_rs.at[j], partner).wait_send()

        @pl.when(j < z)
        def _():
            send(zs.at[j], zr.at[j], z_ss.at[j], z_rs.at[j], partner).wait_send()


def store_kernel(a_ref, b_ref, c_ref, a_out, b_out, c_out, sems):
    copies = [
        pltpu.make_async_copy(src, dst, sems.at[n])
        for n, (src, dst) in enumerate(((c_ref, c_out), (a_ref, a_out), (b_ref, b_out)))
    ]
    for copy in copies:
        copy.start()
    for copy in copies:
        copy.wait()


def body(
    queries, keyvals, d_attn, grad_tokens, expert_ids, route_weights, saved_gate_up, down_weight
):
    dma = pltpu.SemaphoreType.DMA
    vmem = pltpu.VMEM
    shapes = (
        jax.ShapeDtypeStruct((ROWS, HEAD), BF16),
        jax.ShapeDtypeStruct((2, 4, 2 * HEAD), F32),
        jax.ShapeDtypeStruct((1, 1, SLOTS, 2 * FF), BF16),
    )
    outs = pl.pallas_call(
        kernel,
        out_shape=shapes,
        in_specs=[pl.BlockSpec(memory_space=pl.ANY)] * 8,
        out_specs=tuple([pl.BlockSpec(memory_space=pl.ANY)] * 3),
        scratch_shapes=[
            vmem((ROWS, HEAD), BF16),
            vmem((2, 4, 2 * HEAD), F32),
            vmem((SLOTS, 2 * FF), BF16),
            vmem((2, ROWS, HEAD), BF16),
            vmem((NZ, 2, SUB, HEAD), BF16),
            vmem((2, NP, ROWS, HEAD), BF16),
            vmem((NP, KEYS, ROWS), F32),
            vmem((NP, KEYS, ROWS), F32),
            vmem((KEYS, QUERIES), BF16),
            vmem((KEYS, QUERIES), BF16),
            vmem((NP, 3 * NP, ROWS), F32),
            vmem((NP, HEAD, ROWS), BF16),
            vmem((NP, HEAD, ROWS), BF16),
            vmem((NZ, SUB, 2 * HEAD), BF16),
            vmem((NZ, SUB, 2 * HEAD), BF16),
            vmem((NP, 2, 2 * HEAD), F32),
            vmem((NP, 2, 2 * HEAD), F32),
            vmem((8, WIDTH), BF16),
            vmem((8, 8), I32),
            vmem((8, 8), F32),
            vmem((SLOTS, 2 * FF), BF16),
            vmem((FF, WIDTH), BF16),
            vmem((NP, 16, SIDE + EXTRA), BF16),
            vmem((2, 2, SLOTS, SLOTS), BF16),
            vmem((2, SLOTS, SIDE), BF16),
            vmem((2, SLOTS, SIDE), BF16),
            dma((8,)),
        ]
        + [dma((n,)) for n in (NZ, NZ, NP, NP, NP, NP, NP, NP, NZ, NZ, NP, NP)]
        + [dma((2, NP))] * 4,
        compiler_params=pltpu.CompilerParams(
            collective_id=0, has_side_effects=True, vmem_limit_bytes=60 * 1024 * 1024
        ),
        name="layer_backward",
    )(
        queries, keyvals, d_attn, grad_tokens, expert_ids, route_weights, saved_gate_up, down_weight
    )
    return pl.pallas_call(
        store_kernel,
        out_shape=shapes,
        in_specs=[pl.BlockSpec(memory_space=vmem)] * 3,
        out_specs=tuple([pl.BlockSpec(memory_space=pl.ANY)] * 3),
        scratch_shapes=[dma((3,))],
        name="store",
    )(*outs)


def solution(mesh):
    placed = (
        P("ctx", "exp"),
        P(None, "ctx", None),
        P("ctx", "exp"),
        P(("ctx", "exp"), None),
        P(("ctx", "exp"), None),
        P(("ctx", "exp"), None),
        P("ctx", "exp", None, None),
        P("exp", None, None),
    )
    return jax.shard_map(
        body,
        mesh=mesh,
        in_specs=placed,
        out_specs=(P("ctx", "exp"), P(("ctx", "exp"), None, None), P("ctx", "exp", None, None)),
        check_vma=False,
    )
```

```python
import math

import jax
import jax.numpy as jnp
from jax import lax
from jax.experimental import pallas as pl
from jax.experimental.pallas import tpu as pltpu
from jax.sharding import PartitionSpec as P

MESH = pl.DeviceIdType.MESH
F32, BF16, I32 = jnp.float32, jnp.bfloat16, jnp.int32

NZ = 16
NP = 8
ROWS = 128
HEAD = 128
SUB = ROWS // NP
KEYS = NZ * SUB
QUERIES = NP * ROWS
FF = 768
WIDTH = 4096
SIDE = WIDTH // 2
EXTRA = 128
CUT = SIDE // 2
SLOTS = 128
MASKED = -1e30
LATE = 8

contract_last = (((1,), (1,)), ((), ()))


def send(src, dst, ss, rs, device):
    return pltpu.make_async_remote_copy(
        src_ref=src, dst_ref=dst, send_sem=ss, recv_sem=rs, device_id=device, device_id_type=MESH
    )


def choices(ids, weights):
    ids = ids.astype(F32)
    token = lax.broadcasted_iota(I32, (8, 8), 0)
    slot = jnp.zeros((8, 8), F32)
    for t in range(7):
        for k in range(8):
            slot += jnp.where((ids[t : t + 1, k : k + 1] == ids) & (token > t), 1.0, 0.0)
    high = weights.astype(BF16)
    low = (weights - high.astype(F32)).astype(BF16)
    at = lax.broadcasted_iota(I32, (8, EXTRA), 1) - lax.broadcasted_iota(I32, (8, EXTRA), 0)
    out = jnp.zeros((8, EXTRA), F32)
    for n, part in enumerate(((ids * 2.0 + slot).astype(BF16), high, low)):
        spread = jnp.where(at == 8 * n, 1.0, 0.0).astype(BF16)
        out += jnp.dot(part, spread, preferred_element_type=F32)
    return out


def kernel(
    q_ref, kv_ref, do_ref, tok_ref, ids_ref, wts_ref, saved_ref, down_ref,
    dq_hbm, dkv_hbm, dgu_hbm,
    dq_out, dkv_out, dgu_out, block, kv, qd, pun, dps, pb, sb, stats, dqs, dqr, zs, zr, fs, fr,
    tok_v, ids_v, wts_v, saved_v, down_v, tb, placers, outgoing, incoming,
    loc, kv_ss, kv_rs, x_ss, x_rs, st_ss, st_rs, dq_ss, dq_rs,
    z_ss, z_rs, f_ss, f_rs, t_ss, t_rs, a_ss, a_rs,
):
    z, e = lax.axis_index("ctx"), lax.axis_index("exp")
    d = lax.rem(e, NP)
    y = e // NP
    g = y // 2
    scale = 1.0 / math.sqrt(HEAD)

    def row(k):
        other = lax.rem(d + k, NP)
        return other, {"ctx": z, "exp": y * NP + other}

    def column(k):
        other = lax.rem(y + k, NP)
        return other, {"ctx": z, "exp": other * NP + d}

    partner = {"ctx": z, "exp": e + 1 - 2 * lax.rem(e, 2)}
    order = (4, 5, 3, 2, 6, 7, 1)
    cuts = (pl.ds(0, EXTRA + CUT), pl.ds(EXTRA + CUT, CUT))
    own = pl.ds(pl.multiple_of(d * 16, 16), 16)

    kv[...] = jnp.zeros_like(kv)
    zr[...] = jnp.zeros_like(zr)
    barrier = pltpu.get_barrier_semaphore()

    @pl.loop(0, NZ - 1)
    def _(k):
        at = lax.rem(z + 8 + k + k // 8, NZ)
        pl.semaphore_signal(barrier, inc=1, device_id={"ctx": at, "exp": e}, device_id_type=MESH)

    for k in range(1, NP):
        for _, device in (row(k), column(k)):
            pl.semaphore_signal(barrier, inc=1, device_id=device, device_id_type=MESH)

    local = [
        pltpu.make_async_copy(kv_ref.at[:, :, pl.ds(g * HEAD, HEAD)], block, loc.at[0]),
        pltpu.make_async_copy(q_ref, qd.at[0, d], loc.at[1]),
        pltpu.make_async_copy(do_ref, qd.at[1, d], loc.at[2]),
        pltpu.make_async_copy(tok_ref, tok_v, loc.at[3]),
        pltpu.make_async_copy(ids_ref, ids_v, loc.at[4]),
        pltpu.make_async_copy(wts_ref, wts_v, loc.at[5]),
        pltpu.make_async_copy(saved_ref.at[0, 0], saved_v, loc.at[6]),
        pltpu.make_async_copy(down_ref.at[0], down_v, loc.at[7]),
    ]
    for copy in local:
        copy.start()

    local[0].wait()
    near = lax.broadcasted_iota(I32, (SUB, ROWS), 0)
    far = lax.broadcasted_iota(I32, (SUB, ROWS), 1)
    chosen = (far == (near // 2) * SUB + 2 * d + lax.rem(near, 2)).astype(F32).astype(BF16)
    for n in range(2):
        kv[z, n] = jnp.dot(chosen, block[n], preferred_element_type=F32).astype(BF16)

    for copy in local[3:6]:
        copy.wait()
    wide = tok_v[...].astype(F32)
    tb[y, :, EXTRA:] = jnp.concatenate([wide[:, :SIDE], wide[:, SIDE:]], axis=0).astype(BF16)
    beside = choices(ids_v[...], wts_v[...])
    tb[y, :, :EXTRA] = jnp.concatenate([beside, beside], axis=0).astype(BF16)
    for copy in local[1:3]:
        copy.wait()

    pl.semaphore_wait(barrier, NZ - 1 + 2 * (NP - 1))

    @pl.loop(1, NZ)
    def _(k):
        to = z + jnp.where(k <= 8, 9 - k, k)

        @pl.when(to < NZ)
        def _():
            send(kv.at[z], kv.at[z], kv_ss.at[to], kv_rs.at[z], {"ctx": to, "exp": e}).start()

    sends = []

    def start(copy):
        copy.start()
        sends.append(copy)

    for k in (4, 2, 6):
        _, device = row(k)
        start(send(qd.at[:, d], qd.at[:, d], x_ss.at[k], x_rs.at[d], device))
    start(send(qd.at[:, d], qd.at[:, d], x_ss.at[1], x_rs.at[d], partner))
    def send_tokens():
        for n, cut in enumerate(cuts):
            for k in order:
                _, device = column(k)
                mine = tb.at[y, :, cut]
                send(mine, mine, t_ss.at[n, k], t_rs.at[n, y], device).start()

    late = z >= LATE
    pl.when(jnp.logical_not(late))(send_tokens)

    for k in (2, 6, 4):
        other, _ = row(k)
        theirs = qd.at[:, other]
        send(theirs, theirs, x_ss.at[k], x_rs.at[other], partner).wait_recv()
        start(send(theirs, theirs, x_ss.at[k - 1 if k > 2 else 7], x_rs.at[other], partner))
    twin = d + 1 - 2 * lax.rem(d, 2)
    for k in range(0, NP, 2):
        other = lax.rem(twin + k, NP)
        theirs = qd.at[:, other]
        send(theirs, theirs, x_ss.at[0], x_rs.at[other], partner).wait_recv()

    @pl.loop(0, NZ)
    def _(j):
        @pl.when(j < z)
        def _():
            send(kv.at[j], kv.at[j], kv_ss.at[j], kv_rs.at[j], partner).wait_recv()

    keys = kv[:, 0].reshape(KEYS, HEAD)
    values = kv[:, 1].reshape(KEYS, HEAD)
    at = lax.broadcasted_iota(I32, (KEYS, ROWS), 0)
    in_block = lax.rem(at, SUB)
    key_pos = (at // SUB) * ROWS + (in_block // 2) * SUB + 2 * d + lax.rem(in_block, 2)
    causal = key_pos <= z * ROWS + lax.broadcasted_iota(I32, (KEYS, ROWS), 1)
    for h in range(NP):
        s = lax.dot_general(keys, qd[0, h], contract_last, preferred_element_type=F32) * scale
        s = jnp.where(causal, s, MASKED)
        m = jnp.max(s, axis=0, keepdims=True)
        p = jnp.exp(s - m)
        v = lax.dot_general(values, qd[1, h], contract_last, preferred_element_type=F32)
        pun[h] = p
        dps[h] = v
        stats[d, pl.ds(h, 1)] = m
        stats[d, pl.ds(NP + h, 1)] = jnp.sum(p, axis=0, keepdims=True)
        stats[d, pl.ds(2 * NP + h, 1)] = jnp.sum(p * v, axis=0, keepdims=True)
    for k in order:
        _, device = row(k)
        start(send(stats.at[d], stats.at[d], st_ss.at[k], st_rs.at[d], device))

    def await_tokens(n):
        for k in range(1, NP):
            other, _ = column(k)
            theirs = tb.at[other, :, cuts[n]]
            send(theirs, theirs, t_ss.at[n, k], t_rs.at[n, other], partner).wait_recv()

    r = lax.broadcasted_iota(I32, (SLOTS, SLOTS), 0)
    q = lax.broadcasted_iota(I32, (SLOTS, SLOTS), 1)

    def pack(n):
        for half in range(2):
            for m in range(2):
                at = EXTRA + n * CUT + m * 512
                part = tb[:, :, at : at + 512].reshape(SLOTS, 512)
                outgoing[n, :, half * CUT + m * 512 : half * CUT + (m + 1) * 512] = (
                    jnp.dot(placers[0, half], part, preferred_element_type=F32)
                    + jnp.dot(placers[1, half], part, preferred_element_type=F32)
                ).astype(BF16)
        for k in order:
            other, device = row(k)
            theirs = pl.ds(pl.multiple_of(other * 16, 16), 16)
            (
                send(
                    outgoing.at[n, theirs], incoming.at[n, own], a_ss.at[n, k], a_rs.at[n, d], device
                )
            ).start()
        pltpu.make_async_copy(outgoing.at[n, own], incoming.at[n, own], loc.at[n]).start()

    def first_part():
        await_tokens(0)
        beside = tb[:, :, :EXTRA].reshape(SLOTS, EXTRA).astype(F32).T
        wanted = ((y * NP + r // 16) * 2 + lax.rem(r, 2)).astype(F32)
        same = lax.rem(r, 16) // 2 == q // 16
        high = jnp.zeros((SLOTS, SLOTS), F32)
        low = jnp.zeros((SLOTS, SLOTS), F32)
        for k in range(8):
            hit = same & (beside[k : k + 1] == wanted)
            high += jnp.where(hit, beside[8 + k : 9 + k], 0.0)
            low += jnp.where(hit, beside[16 + k : 17 + k], 0.0)
        first = lax.rem(q, 16) < 8
        for n, part in enumerate((high, low)):
            placers[n, 0] = jnp.where(first, part, 0.0).astype(BF16)
            placers[n, 1] = jnp.where(first, 0.0, part).astype(BF16)
        pack(0)

    pl.when(jnp.logical_not(late))(first_part)

    for k in range(1, NP):
        other, _ = row(k)
        send(stats.at[other], stats.at[other], st_ss.at[k], st_rs.at[other], partner).wait_recv()

    pl.when(late)(send_tokens)

    top = stats[0, 0:NP]
    for n in range(1, NP):
        top = jnp.maximum(top, stats[n, 0:NP])
    shifts = [jnp.exp(stats[n, 0:NP] - top) for n in range(NP)]
    mass = sum(stats[n, NP : 2 * NP] * shifts[n] for n in range(NP))
    delta = sum(stats[n, 2 * NP : 3 * NP] * shifts[n] for n in range(NP)) / mass
    factor = jnp.exp(stats[d, 0:NP] - (top + jnp.log(mass)))
    for h in range(NP):
        p = pun[h] * factor[h : h + 1]
        pb[:, h * ROWS : (h + 1) * ROWS] = p.astype(BF16)
        sb[:, h * ROWS : (h + 1) * ROWS] = (p * (dps[h] - delta[h : h + 1])).astype(BF16)
    dk = jnp.dot(sb[...], qd[0].reshape(QUERIES, HEAD), preferred_element_type=F32) * scale
    zs[:, :, :HEAD] = dk.astype(BF16).reshape(NZ, SUB, HEAD)
    dv = jnp.dot(pb[...], qd[1].reshape(QUERIES, HEAD), preferred_element_type=F32)
    zs[:, :, HEAD:] = dv.astype(BF16).reshape(NZ, SUB, HEAD)

    @pl.loop(0, NZ)
    def _(j):
        @pl.when(j < z)
        def _():
            send(zs.at[j], zr.at[z], z_ss.at[j], z_rs.at[z], {"ctx": j, "exp": e}).start()

    keys_t = keys.astype(F32).T.astype(BF16)
    for h in range(NP):
        dqs[h] = (
            jnp.dot(keys_t, sb[:, h * ROWS : (h + 1) * ROWS], preferred_element_type=F32) * scale
        ).astype(BF16)
    for k in order:
        other, device = row(k)
        start(send(dqs.at[other], dqr.at[d], dq_ss.at[k], dq_rs.at[d], device))

    pl.when(late)(first_part)
    await_tokens(1)
    pack(1)

    for copy in local[6:]:
        copy.wait()
    swap = (lax.rem(r, 16) // 2 == q // 16) & (r // 16 == lax.rem(q, 16) // 2)
    swap = (swap & (lax.rem(r, 2) == lax.rem(q, 2))).astype(F32).astype(BF16)

    def down_part(n):
        pltpu.make_async_copy(outgoing.at[n, own], incoming.at[n, own], loc.at[n]).wait()
        for k in range(1, NP):
            other, _ = row(k)
            theirs = pl.ds(pl.multiple_of(other * 16, 16), 16)
            send(
                outgoing.at[n, own], incoming.at[n, theirs], a_ss.at[n, k], a_rs.at[n, other], partner
            ).wait_recv()
        total = jnp.zeros((SLOTS, FF), F32)
        for half in range(2):
            part = incoming[n, :, half * CUT : (half + 1) * CUT]
            rows = jnp.dot(swap, part, preferred_element_type=F32).astype(BF16)
            at = half * SIDE + n * CUT
            total += lax.dot_general(
                rows, down_v[:, at : at + CUT], contract_last, preferred_element_type=F32
            )
        return total

    hidden = down_part(0)

    @pl.loop(0, NZ)
    def _(j):
        @pl.when(j > z)
        def _():
            send(zs.at[j], zr.at[j], z_ss.at[j], z_rs.at[j], partner).wait_recv()

    summed = zs[z].astype(F32)
    for n in range(NZ):
        summed += zr[n].astype(F32)
    for n in range(NP):
        fs[n] = summed[2 * n : 2 * n + 2]
    fr[y] = fs[y]
    last = []
    for k in range(1, NP):
        other, device = column(k)
        last.append(send(fs.at[other], fr.at[y], f_ss.at[k], f_rs.at[y], device))
        last[-1].start()

    dq = dqs[d].astype(F32)
    for k in range(1, NP):
        other, _ = row(k)
        send(dqs.at[other], dqr.at[other], dq_ss.at[k], dq_rs.at[other], partner).wait_recv()
        dq += dqr[other].astype(F32)
    dq_out[...] = dq.T.astype(BF16)
    written = [pltpu.make_async_copy(dq_out, dq_hbm, loc.at[2])]
    written[-1].start()

    hidden += down_part(1)
    gate = saved_v[:, :FF].astype(F32)
    up = saved_v[:, FF:].astype(F32)
    sig = 1.0 / (1.0 + jnp.exp(-gate))
    dgu_out[:, :FF] = (hidden * up * sig * (1.0 + gate * (1.0 - sig))).astype(BF16)
    dgu_out[:, FF:] = (hidden * gate * sig).astype(BF16)
    written.append(pltpu.make_async_copy(dgu_out, dgu_hbm.at[0, 0], loc.at[3]))
    written[-1].start()

    for copy in sends:
        copy.wait_send()
    for n, cut in enumerate(cuts):
        for k in order:
            mine = tb.at[y, :, cut]
            send(mine, mine, t_ss.at[n, k], t_rs.at[n, y], partner).wait_send()
            send(
                outgoing.at[n, own], incoming.at[n, own], a_ss.at[n, k], a_rs.at[n, d], partner
            ).wait_send()

    @pl.loop(0, NZ)
    def _(j):
        @pl.when(j > z)
        def _():
            send(kv.at[z], kv.at[z], kv_ss.at[j], kv_rs.at[j], partner).wait_send()

        @pl.when(j < z)
        def _():
            send(zs.at[j], zr.at[j], z_ss.at[j], z_rs.at[j], partner).wait_send()

    for k in range(1, NP):
        other, _ = column(k)
        send(fs.at[other], fr.at[other], f_ss.at[k], f_rs.at[other], partner).wait_recv()
    for n in range(4):
        dkv_out[:, n, :] = fr[2 * n] + fr[2 * n + 1]
    written.append(pltpu.make_async_copy(dkv_out, dkv_hbm, loc.at[4]))
    written[-1].start()
    for copy in last:
        copy.wait_send()
    for copy in written:
        copy.wait()


def store_kernel(a_ref, b_ref, c_ref, a_out, b_out, c_out, a_v, b_v, c_v, sems):
    half = [pl.ds(n * SLOTS // 2, SLOTS // 2) for n in range(2)]
    steps = [(c_ref.at[0, 0, h], c_v.at[h], c_out.at[0, 0, h]) for h in half]
    steps += [(a_ref, a_v, a_out), (b_ref, b_v, b_out)]
    loads = [pltpu.make_async_copy(s[0], s[1], sems.at[n]) for n, s in enumerate(steps)]
    stores = [pltpu.make_async_copy(s[1], s[2], sems.at[4 + n]) for n, s in enumerate(steps)]
    for copy in loads:
        copy.start()
    for load, store in zip(loads, stores):
        load.wait()
        store.start()
    for copy in stores:
        copy.wait()


def body(
    queries, keyvals, d_attn, grad_tokens, expert_ids, route_weights, saved_gate_up, down_weight
):
    dma = pltpu.SemaphoreType.DMA
    vmem = pltpu.VMEM
    shapes = (
        jax.ShapeDtypeStruct((ROWS, HEAD), BF16),
        jax.ShapeDtypeStruct((2, 4, 2 * HEAD), F32),
        jax.ShapeDtypeStruct((1, 1, SLOTS, 2 * FF), BF16),
    )
    outs = pl.pallas_call(
        kernel,
        out_shape=shapes,
        in_specs=[pl.BlockSpec(memory_space=pl.ANY)] * 8,
        out_specs=tuple([pl.BlockSpec(memory_space=pl.ANY)] * 3),
        scratch_shapes=[
            vmem((ROWS, HEAD), BF16),
            vmem((2, 4, 2 * HEAD), F32),
            vmem((SLOTS, 2 * FF), BF16),
            vmem((2, ROWS, HEAD), BF16),
            vmem((NZ, 2, SUB, HEAD), BF16),
            vmem((2, NP, ROWS, HEAD), BF16),
            vmem((NP, KEYS, ROWS), F32),
            vmem((NP, KEYS, ROWS), F32),
            vmem((KEYS, QUERIES), BF16),
            vmem((KEYS, QUERIES), BF16),
            vmem((NP, 3 * NP, ROWS), F32),
            vmem((NP, HEAD, ROWS), BF16),
            vmem((NP, HEAD, ROWS), BF16),
            vmem((NZ, SUB, 2 * HEAD), BF16),
            vmem((NZ, SUB, 2 * HEAD), BF16),
            vmem((NP, 2, 2 * HEAD), F32),
            vmem((NP, 2, 2 * HEAD), F32),
            vmem((8, WIDTH), BF16),
            vmem((8, 8), I32),
            vmem((8, 8), F32),
            vmem((SLOTS, 2 * FF), BF16),
            vmem((FF, WIDTH), BF16),
            vmem((NP, 16, SIDE + EXTRA), BF16),
            vmem((2, 2, SLOTS, SLOTS), BF16),
            vmem((2, SLOTS, SIDE), BF16),
            vmem((2, SLOTS, SIDE), BF16),
            dma((8,)),
        ]
        + [dma((n,)) for n in (NZ, NZ, NP, NP, NP, NP, NP, NP, NZ, NZ, NP, NP)]
        + [dma((2, NP))] * 4,
        compiler_params=pltpu.CompilerParams(
            collective_id=0, has_side_effects=True, vmem_limit_bytes=60 * 1024 * 1024
        ),
        name="layer_backward",
    )(
        queries, keyvals, d_attn, grad_tokens, expert_ids, route_weights, saved_gate_up, down_weight
    )
    return pl.pallas_call(
        store_kernel,
        out_shape=shapes,
        in_specs=[pl.BlockSpec(memory_space=pl.ANY)] * 3,
        out_specs=tuple([pl.BlockSpec(memory_space=pl.ANY)] * 3),
        scratch_shapes=[
            vmem((ROWS, HEAD), BF16),
            vmem((2, 4, 2 * HEAD), F32),
            vmem((SLOTS, 2 * FF), BF16),
            dma((8,)),
        ],
        compiler_params=pltpu.CompilerParams(vmem_limit_bytes=60 * 1024 * 1024),
        name="store",
    )(*outs)


def solution(mesh):
    placed = (
        P("ctx", "exp"),
        P(None, "ctx", None),
        P("ctx", "exp"),
        P(("ctx", "exp"), None),
        P(("ctx", "exp"), None),
        P(("ctx", "exp"), None),
        P("ctx", "exp", None, None),
        P("exp", None, None),
    )
    return jax.shard_map(
        body,
        mesh=mesh,
        in_specs=placed,
        out_specs=(P("ctx", "exp"), P(("ctx", "exp"), None, None), P("ctx", "exp", None, None)),
        check_vma=False,
    )
```

```python
import math

import jax
import jax.numpy as jnp
from jax import lax
from jax.experimental import pallas as pl
from jax.experimental.pallas import tpu as pltpu
from jax.sharding import PartitionSpec as P

MESH = pl.DeviceIdType.MESH
F32, BF16, I32 = jnp.float32, jnp.bfloat16, jnp.int32

NZ = 16
NP = 8
ROWS = 128
HEAD = 128
SUB = ROWS // NP
KEYS = NZ * SUB
QUERIES = NP * ROWS
FF = 768
WIDTH = 4096
SIDE = WIDTH // 2
EXTRA = 128
CUT = SIDE // 2
SLOTS = 128
MASKED = -1e30
LATE = 8

contract_last = (((1,), (1,)), ((), ()))


def send(src, dst, ss, rs, device):
    return pltpu.make_async_remote_copy(
        src_ref=src, dst_ref=dst, send_sem=ss, recv_sem=rs, device_id=device, device_id_type=MESH
    )


def choices(ids, weights):
    ids = ids.astype(F32)
    token = lax.broadcasted_iota(I32, (8, 8), 0)
    slot = jnp.zeros((8, 8), F32)
    for t in range(7):
        for k in range(8):
            slot += jnp.where((ids[t : t + 1, k : k + 1] == ids) & (token > t), 1.0, 0.0)
    high = weights.astype(BF16)
    low = (weights - high.astype(F32)).astype(BF16)
    at = lax.broadcasted_iota(I32, (8, EXTRA), 1) - lax.broadcasted_iota(I32, (8, EXTRA), 0)
    out = jnp.zeros((8, EXTRA), F32)
    for n, part in enumerate(((ids * 2.0 + slot).astype(BF16), high, low)):
        spread = jnp.where(at == 8 * n, 1.0, 0.0).astype(BF16)
        out += jnp.dot(part, spread, preferred_element_type=F32)
    return out


def kernel(
    q_ref, kv_ref, do_ref, tok_ref, ids_ref, wts_ref, saved_ref, down_ref,
    dq_hbm, dkv_hbm, dgu_hbm,
    dq_out, dkv_out, dgu_out, block, kv, qd, pun, dps, pb, sb, stats, dqs, dqr, zs, zr, fs, fr,
    tok_v, ids_v, wts_v, saved_v, down_v, tb, placers, outgoing, incoming,
    loc, kv_ss, kv_rs, x_ss, x_rs, st_ss, st_rs, dq_ss, dq_rs,
    z_ss, z_rs, f_ss, f_rs, t_ss, t_rs, a_ss, a_rs,
):
    z, e = lax.axis_index("ctx"), lax.axis_index("exp")
    d = lax.rem(e, NP)
    y = e // NP
    g = y // 2
    scale = 1.0 / math.sqrt(HEAD)

    def row(k):
        other = lax.rem(d + k, NP)
        return other, {"ctx": z, "exp": y * NP + other}

    def column(k):
        other = lax.rem(y + k, NP)
        return other, {"ctx": z, "exp": other * NP + d}

    partner = {"ctx": z, "exp": e + 1 - 2 * lax.rem(e, 2)}
    order = (4, 5, 3, 2, 6, 7, 1)
    cuts = (pl.ds(0, EXTRA + CUT), pl.ds(EXTRA + CUT, CUT))
    own = pl.ds(pl.multiple_of(d * 16, 16), 16)

    kv[...] = jnp.zeros_like(kv)
    zr[...] = jnp.zeros_like(zr)
    barrier = pltpu.get_barrier_semaphore()

    @pl.loop(0, NZ - 1)
    def _(k):
        at = lax.rem(z + 8 + k + k // 8, NZ)
        pl.semaphore_signal(barrier, inc=1, device_id={"ctx": at, "exp": e}, device_id_type=MESH)

    for k in range(1, NP):
        for _, device in (row(k), column(k)):
            pl.semaphore_signal(barrier, inc=1, device_id=device, device_id_type=MESH)

    local = [
        pltpu.make_async_copy(kv_ref.at[:, :, pl.ds(g * HEAD, HEAD)], block, loc.at[0]),
        pltpu.make_async_copy(q_ref, qd.at[0, d], loc.at[1]),
        pltpu.make_async_copy(do_ref, qd.at[1, d], loc.at[2]),
        pltpu.make_async_copy(tok_ref, tok_v, loc.at[3]),
        pltpu.make_async_copy(ids_ref, ids_v, loc.at[4]),
        pltpu.make_async_copy(wts_ref, wts_v, loc.at[5]),
        pltpu.make_async_copy(saved_ref.at[0, 0], saved_v, loc.at[6]),
        pltpu.make_async_copy(down_ref.at[0], down_v, loc.at[7]),
    ]
    for copy in local:
        copy.start()

    local[0].wait()
    near = lax.broadcasted_iota(I32, (SUB, ROWS), 0)
    far = lax.broadcasted_iota(I32, (SUB, ROWS), 1)
    chosen = (far == (near // 2) * SUB + 2 * d + lax.rem(near, 2)).astype(F32).astype(BF16)
    for n in range(2):
        kv[z, n] = jnp.dot(chosen, block[n], preferred_element_type=F32).astype(BF16)

    for copy in local[3:6]:
        copy.wait()
    wide = tok_v[...].astype(F32)
    tb[y, :, EXTRA:] = jnp.concatenate([wide[:, :SIDE], wide[:, SIDE:]], axis=0).astype(BF16)
    beside = choices(ids_v[...], wts_v[...])
    tb[y, :, :EXTRA] = jnp.concatenate([beside, beside], axis=0).astype(BF16)
    for copy in local[1:3]:
        copy.wait()

    pl.semaphore_wait(barrier, NZ - 1 + 2 * (NP - 1))

    @pl.loop(1, NZ)
    def _(k):
        to = z + jnp.where(k <= 8, 9 - k, k)

        @pl.when(to < NZ)
        def _():
            send(kv.at[z], kv.at[z], kv_ss.at[to], kv_rs.at[z], {"ctx": to, "exp": e}).start()

    sends = []

    def start(copy):
        copy.start()
        sends.append(copy)

    for k in (4, 2, 6):
        _, device = row(k)
        start(send(qd.at[:, d], qd.at[:, d], x_ss.at[k], x_rs.at[d], device))
    start(send(qd.at[:, d], qd.at[:, d], x_ss.at[1], x_rs.at[d], partner))
    def send_tokens():
        for n, cut in enumerate(cuts):
            for k in order:
                _, device = column(k)
                mine = tb.at[y, :, cut]
                send(mine, mine, t_ss.at[n, k], t_rs.at[n, y], device).start()

    late = z >= LATE
    pl.when(jnp.logical_not(late))(send_tokens)

    for k in (2, 6, 4):
        other, _ = row(k)
        theirs = qd.at[:, other]
        send(theirs, theirs, x_ss.at[k], x_rs.at[other], partner).wait_recv()
        start(send(theirs, theirs, x_ss.at[k - 1 if k > 2 else 7], x_rs.at[other], partner))
    twin = d + 1 - 2 * lax.rem(d, 2)
    for k in range(0, NP, 2):
        other = lax.rem(twin + k, NP)
        theirs = qd.at[:, other]
        send(theirs, theirs, x_ss.at[0], x_rs.at[other], partner).wait_recv()

    @pl.loop(0, NZ)
    def _(j):
        @pl.when(j < z)
        def _():
            send(kv.at[j], kv.at[j], kv_ss.at[j], kv_rs.at[j], partner).wait_recv()

    keys = kv[:, 0].reshape(KEYS, HEAD)
    values = kv[:, 1].reshape(KEYS, HEAD)
    at = lax.broadcasted_iota(I32, (KEYS, ROWS), 0)
    in_block = lax.rem(at, SUB)
    key_pos = (at // SUB) * ROWS + (in_block // 2) * SUB + 2 * d + lax.rem(in_block, 2)
    causal = key_pos <= z * ROWS + lax.broadcasted_iota(I32, (KEYS, ROWS), 1)
    for h in range(NP):
        s = lax.dot_general(keys, qd[0, h], contract_last, preferred_element_type=F32) * scale
        s = jnp.where(causal, s, MASKED)
        m = jnp.max(s, axis=0, keepdims=True)
        p = jnp.exp(s - m)
        v = lax.dot_general(values, qd[1, h], contract_last, preferred_element_type=F32)
        pun[h] = p
        dps[h] = v
        stats[d, pl.ds(h, 1)] = m
        stats[d, pl.ds(NP + h, 1)] = jnp.sum(p, axis=0, keepdims=True)
        stats[d, pl.ds(2 * NP + h, 1)] = jnp.sum(p * v, axis=0, keepdims=True)
    for k in order:
        _, device = row(k)
        start(send(stats.at[d], stats.at[d], st_ss.at[k], st_rs.at[d], device))

    def await_tokens(n):
        for k in range(1, NP):
            other, _ = column(k)
            theirs = tb.at[other, :, cuts[n]]
            send(theirs, theirs, t_ss.at[n, k], t_rs.at[n, other], partner).wait_recv()

    r = lax.broadcasted_iota(I32, (SLOTS, SLOTS), 0)
    q = lax.broadcasted_iota(I32, (SLOTS, SLOTS), 1)

    def pack(n):
        for half in range(2):
            for m in range(2):
                at = EXTRA + n * CUT + m * 512
                part = tb[:, :, at : at + 512].reshape(SLOTS, 512)
                outgoing[n, :, half * CUT + m * 512 : half * CUT + (m + 1) * 512] = (
                    jnp.dot(placers[0, half], part, preferred_element_type=F32)
                    + jnp.dot(placers[1, half], part, preferred_element_type=F32)
                ).astype(BF16)
        for k in order:
            other, device = row(k)
            theirs = pl.ds(pl.multiple_of(other * 16, 16), 16)
            (
                send(
                    outgoing.at[n, theirs], incoming.at[n, own], a_ss.at[n, k], a_rs.at[n, d], device
                )
            ).start()
        pltpu.make_async_copy(outgoing.at[n, own], incoming.at[n, own], loc.at[n]).start()

    def first_part():
        await_tokens(0)
        beside = tb[:, :, :EXTRA].reshape(SLOTS, EXTRA).astype(F32).T
        wanted = ((y * NP + r // 16) * 2 + lax.rem(r, 2)).astype(F32)
        same = lax.rem(r, 16) // 2 == q // 16
        high = jnp.zeros((SLOTS, SLOTS), F32)
        low = jnp.zeros((SLOTS, SLOTS), F32)
        for k in range(8):
            hit = same & (beside[k : k + 1] == wanted)
            high += jnp.where(hit, beside[8 + k : 9 + k], 0.0)
            low += jnp.where(hit, beside[16 + k : 17 + k], 0.0)
        first = lax.rem(q, 16) < 8
        for n, part in enumerate((high, low)):
            placers[n, 0] = jnp.where(first, part, 0.0).astype(BF16)
            placers[n, 1] = jnp.where(first, 0.0, part).astype(BF16)
        pack(0)

    pl.when(jnp.logical_not(late))(first_part)

    for k in range(1, NP):
        other, _ = row(k)
        send(stats.at[other], stats.at[other], st_ss.at[k], st_rs.at[other], partner).wait_recv()

    pl.when(late)(send_tokens)

    top = stats[0, 0:NP]
    for n in range(1, NP):
        top = jnp.maximum(top, stats[n, 0:NP])
    shifts = [jnp.exp(stats[n, 0:NP] - top) for n in range(NP)]
    mass = sum(stats[n, NP : 2 * NP] * shifts[n] for n in range(NP))
    delta = sum(stats[n, 2 * NP : 3 * NP] * shifts[n] for n in range(NP)) / mass
    factor = jnp.exp(stats[d, 0:NP] - (top + jnp.log(mass)))
    for h in range(NP):
        p = pun[h] * factor[h : h + 1]
        pb[:, h * ROWS : (h + 1) * ROWS] = p.astype(BF16)
        sb[:, h * ROWS : (h + 1) * ROWS] = (p * (dps[h] - delta[h : h + 1])).astype(BF16)
    dk = jnp.dot(sb[...], qd[0].reshape(QUERIES, HEAD), preferred_element_type=F32) * scale
    zs[:, :, :HEAD] = dk.astype(BF16).reshape(NZ, SUB, HEAD)
    dv = jnp.dot(pb[...], qd[1].reshape(QUERIES, HEAD), preferred_element_type=F32)
    zs[:, :, HEAD:] = dv.astype(BF16).reshape(NZ, SUB, HEAD)

    @pl.loop(0, NZ)
    def _(j):
        @pl.when(j < z)
        def _():
            send(zs.at[j], zr.at[z], z_ss.at[j], z_rs.at[z], {"ctx": j, "exp": e}).start()

    keys_t = keys.astype(F32).T.astype(BF16)
    for h in range(NP):
        dqs[h] = (
            jnp.dot(keys_t, sb[:, h * ROWS : (h + 1) * ROWS], preferred_element_type=F32) * scale
        ).astype(BF16)
    for k in order:
        other, device = row(k)
        start(send(dqs.at[other], dqr.at[d], dq_ss.at[k], dq_rs.at[d], device))

    pl.when(late)(first_part)
    await_tokens(1)
    pack(1)

    for copy in local[6:]:
        copy.wait()
    swap = (lax.rem(r, 16) // 2 == q // 16) & (r // 16 == lax.rem(q, 16) // 2)
    swap = (swap & (lax.rem(r, 2) == lax.rem(q, 2))).astype(F32).astype(BF16)

    def down_part(n):
        pltpu.make_async_copy(outgoing.at[n, own], incoming.at[n, own], loc.at[n]).wait()
        for k in range(1, NP):
            other, _ = row(k)
            theirs = pl.ds(pl.multiple_of(other * 16, 16), 16)
            send(
                outgoing.at[n, own], incoming.at[n, theirs], a_ss.at[n, k], a_rs.at[n, other], partner
            ).wait_recv()
        total = jnp.zeros((SLOTS, FF), F32)
        for half in range(2):
            part = incoming[n, :, half * CUT : (half + 1) * CUT]
            rows = jnp.dot(swap, part, preferred_element_type=F32).astype(BF16)
            at = half * SIDE + n * CUT
            total += lax.dot_general(
                rows, down_v[:, at : at + CUT], contract_last, preferred_element_type=F32
            )
        return total


    @pl.loop(0, NZ)
    def _(j):
        @pl.when(j > z)
        def _():
            send(zs.at[j], zr.at[j], z_ss.at[j], z_rs.at[j], partner).wait_recv()

    summed = zs[z].astype(F32)
    for n in range(NZ):
        summed += zr[n].astype(F32)
    for n in range(NP):
        fs[n] = summed[2 * n : 2 * n + 2]
    fr[y] = fs[y]
    last = []
    for k in range(1, NP):
        other, device = column(k)
        last.append(send(fs.at[other], fr.at[y], f_ss.at[k], f_rs.at[y], device))
        last[-1].start()

    dq = dqs[d].astype(F32)
    for k in range(1, NP):
        other, _ = row(k)
        send(dqs.at[other], dqr.at[other], dq_ss.at[k], dq_rs.at[other], partner).wait_recv()
        dq += dqr[other].astype(F32)
    dq_out[...] = dq.T.astype(BF16)
    written = [pltpu.make_async_copy(dq_out, dq_hbm, loc.at[2])]
    written[-1].start()

    hidden = down_part(0) + down_part(1)
    gate = saved_v[:, :FF].astype(F32)
    up = saved_v[:, FF:].astype(F32)
    sig = 1.0 / (1.0 + jnp.exp(-gate))
    dgu_out[:, :FF] = (hidden * up * sig * (1.0 + gate * (1.0 - sig))).astype(BF16)
    dgu_out[:, FF:] = (hidden * gate * sig).astype(BF16)
    written.append(pltpu.make_async_copy(dgu_out, dgu_hbm.at[0, 0], loc.at[3]))
    written[-1].start()

    for copy in sends:
        copy.wait_send()
    for n, cut in enumerate(cuts):
        for k in order:
            mine = tb.at[y, :, cut]
            send(mine, mine, t_ss.at[n, k], t_rs.at[n, y], partner).wait_send()
            send(
                outgoing.at[n, own], incoming.at[n, own], a_ss.at[n, k], a_rs.at[n, d], partner
            ).wait_send()

    @pl.loop(0, NZ)
    def _(j):
        @pl.when(j > z)
        def _():
            send(kv.at[z], kv.at[z], kv_ss.at[j], kv_rs.at[j], partner).wait_send()

        @pl.when(j < z)
        def _():
            send(zs.at[j], zr.at[j], z_ss.at[j], z_rs.at[j], partner).wait_send()

    for k in range(1, NP):
        other, _ = column(k)
        send(fs.at[other], fr.at[other], f_ss.at[k], f_rs.at[other], partner).wait_recv()
    for n in range(4):
        dkv_out[:, n, :] = fr[2 * n] + fr[2 * n + 1]
    written.append(pltpu.make_async_copy(dkv_out, dkv_hbm, loc.at[4]))
    written[-1].start()
    for copy in last:
        copy.wait_send()
    for copy in written:
        copy.wait()


def store_kernel(a_ref, b_ref, c_ref, a_out, b_out, c_out, a_v, b_v, c_v, sems):
    half = [pl.ds(n * SLOTS // 2, SLOTS // 2) for n in range(2)]
    steps = [(c_ref.at[0, 0, h], c_v.at[h], c_out.at[0, 0, h]) for h in half]
    steps += [(a_ref, a_v, a_out), (b_ref, b_v, b_out)]
    loads = [pltpu.make_async_copy(s[0], s[1], sems.at[n]) for n, s in enumerate(steps)]
    stores = [pltpu.make_async_copy(s[1], s[2], sems.at[4 + n]) for n, s in enumerate(steps)]
    for copy in loads:
        copy.start()
    for load, store in zip(loads, stores):
        load.wait()
        store.start()
    for copy in stores:
        copy.wait()


def body(
    queries, keyvals, d_attn, grad_tokens, expert_ids, route_weights, saved_gate_up, down_weight
):
    dma = pltpu.SemaphoreType.DMA
    vmem = pltpu.VMEM
    shapes = (
        jax.ShapeDtypeStruct((ROWS, HEAD), BF16),
        jax.ShapeDtypeStruct((2, 4, 2 * HEAD), F32),
        jax.ShapeDtypeStruct((1, 1, SLOTS, 2 * FF), BF16),
    )
    outs = pl.pallas_call(
        kernel,
        out_shape=shapes,
        in_specs=[pl.BlockSpec(memory_space=pl.ANY)] * 8,
        out_specs=tuple([pl.BlockSpec(memory_space=pl.ANY)] * 3),
        scratch_shapes=[
            vmem((ROWS, HEAD), BF16),
            vmem((2, 4, 2 * HEAD), F32),
            vmem((SLOTS, 2 * FF), BF16),
            vmem((2, ROWS, HEAD), BF16),
            vmem((NZ, 2, SUB, HEAD), BF16),
            vmem((2, NP, ROWS, HEAD), BF16),
            vmem((NP, KEYS, ROWS), F32),
            vmem((NP, KEYS, ROWS), F32),
            vmem((KEYS, QUERIES), BF16),
            vmem((KEYS, QUERIES), BF16),
            vmem((NP, 3 * NP, ROWS), F32),
            vmem((NP, HEAD, ROWS), BF16),
            vmem((NP, HEAD, ROWS), BF16),
            vmem((NZ, SUB, 2 * HEAD), BF16),
            vmem((NZ, SUB, 2 * HEAD), BF16),
            vmem((NP, 2, 2 * HEAD), F32),
            vmem((NP, 2, 2 * HEAD), F32),
            vmem((8, WIDTH), BF16),
            vmem((8, 8), I32),
            vmem((8, 8), F32),
            vmem((SLOTS, 2 * FF), BF16),
            vmem((FF, WIDTH), BF16),
            vmem((NP, 16, SIDE + EXTRA), BF16),
            vmem((2, 2, SLOTS, SLOTS), BF16),
            vmem((2, SLOTS, SIDE), BF16),
            vmem((2, SLOTS, SIDE), BF16),
            dma((8,)),
        ]
        + [dma((n,)) for n in (NZ, NZ, NP, NP, NP, NP, NP, NP, NZ, NZ, NP, NP)]
        + [dma((2, NP))] * 4,
        compiler_params=pltpu.CompilerParams(
            collective_id=0, has_side_effects=True, vmem_limit_bytes=60 * 1024 * 1024
        ),
        name="layer_backward",
    )(
        queries, keyvals, d_attn, grad_tokens, expert_ids, route_weights, saved_gate_up, down_weight
    )
    return pl.pallas_call(
        store_kernel,
        out_shape=shapes,
        in_specs=[pl.BlockSpec(memory_space=pl.ANY)] * 3,
        out_specs=tuple([pl.BlockSpec(memory_space=pl.ANY)] * 3),
        scratch_shapes=[
            vmem((ROWS, HEAD), BF16),
            vmem((2, 4, 2 * HEAD), F32),
            vmem((SLOTS, 2 * FF), BF16),
            dma((8,)),
        ],
        compiler_params=pltpu.CompilerParams(vmem_limit_bytes=60 * 1024 * 1024),
        name="store",
    )(*outs)


def solution(mesh):
    placed = (
        P("ctx", "exp"),
        P(None, "ctx", None),
        P("ctx", "exp"),
        P(("ctx", "exp"), None),
        P(("ctx", "exp"), None),
        P(("ctx", "exp"), None),
        P("ctx", "exp", None, None),
        P("exp", None, None),
    )
    return jax.shard_map(
        body,
        mesh=mesh,
        in_specs=placed,
        out_specs=(P("ctx", "exp"), P(("ctx", "exp"), None, None), P("ctx", "exp", None, None)),
        check_vma=False,
    )
```
